128 devices in a mesh: lon: 16 (over z_lo, x, core), lat: 8 (over y, z_hi).
Axes of the slice: x: 4, y: 4, z: 4 (z_hi: 2, z_lo: 2; z = z_hi * 2 + z_lo), core: 2. Of those that a mesh axis runs over, the one named last changes fastest.
Arguments:
- fields: bfloat16 [192, 384, 3, 512], P('lat', 'lon'), may hold values from -6 to 6
- region_ids: int32 [192], P('lat'), may hold values from 0 to 31, never falling along the last dimension, each value on 1 to 12 neighbouring positions
- w_qkv: bfloat16 [1536, 512], P(('lon', 'lat')), may hold values from -2 to 2
- w_proj: bfloat16 [512, 512], P(('lon', 'lat')), may hold values from -0.25 to 0.25
- grad_output: bfloat16 [192, 384, 3, 512], P('lat', 'lon'), may hold values from -6 to 6
Outputs:
- block_out: bfloat16 [192, 384, 3, 512], P('lat', 'lon')
- grad_fields: bfloat16 [192, 384, 3, 512], P('lat', 'lon')
- grad_w_qkv: float32 [1536, 512], P(('lon', 'lat'))
- grad_w_proj: float32 [512, 512], P(('lon', 'lat'))
The draws below stay inside these ranges and needn't reach their ends.
Inputs may be any that keep to these rules, and one draw needn't show every extreme that they name: `region_ids`: region ids never fall along the rows; each region spans 1 to 12 rows.
All inputs are finite; a program needn't handle non-finite values.
Results may differ from the reference program's by a relative error of at most 0.018.
The reference program's roundings to bfloat16 on the way count: a program that leaves them out, or rounds other values in their place, can miss the bound.
Values may be sent and summed in bfloat16 or wider, within the bound.
A program may use at most 128 MiB of HBM per device.

```python
import math
import jax
import jax.numpy as jnp
import numpy as np
from jax import lax

C = 512
HEADS = 8
HEAD = 64
WIN = 12
LEVELS = 3
NLAT = 192
NLON = 384
TOKENS = 221184


def draw_fields(key, part):
    shape = (NLAT, NLON, LEVELS, C)
    values = jnp.clip(jax.random.normal(jax.random.fold_in(key, 12), shape, jnp.float32), -6.0, 6.0)
    return values.astype(jnp.bfloat16)


def draw_w_qkv(key, part):
    first = jax.random.fold_in(jax.random.fold_in(key, 21), 0)
    whole = jnp.clip(jax.random.normal(first, (3 * C, C), jnp.float32), -6.0, 6.0) * C ** (-0.5)
    return whole.astype(jnp.bfloat16)


def with_spikes(values, stream_key, source, target, blocks, factor):
    owner, partner = [(jnp.arange(values.shape[dim]) // (values.shape[dim] // blocks)).reshape([-1 if axis == dim else 1 for axis in range(values.ndim)]) for dim in (source, target)]
    chosen = jax.random.permutation(stream_key, blocks)[partner]
    strong = (owner == chosen) | (owner == (partner + blocks // 2) % blocks)
    return jnp.where(strong, factor * values, values)


def levels(rng, shape, cuts, smallest, high):
    def one(dim, blocks):
        draws = jax.random.uniform(jax.random.fold_in(jax.random.fold_in(rng, 6), dim), (blocks,), jnp.float32, smallest / len(cuts), high / len(cuts))
        return jnp.repeat(jnp.exp(draws), shape[dim] // blocks).reshape((-1,) + (1,) * (len(shape) - dim - 1))

    level = one(*cuts[0])
    for cut in cuts[1:]:
        level = level * one(*cut)
    return level


def profile(count, total, bound, lean):
    loads = [(1 << 20) // math.isqrt(grade ** lean) + 1 for grade in range(2, count + 1)]
    spare, given = total - bound - (count - 1), [1] * (count - 1)
    while spare > 0:
        movable = [i for i in range(count - 1) if given[i] < bound]
        pool, remaining = sum([loads[i] for i in movable]), spare
        for i in movable:
            extra = min(bound - given[i], max(1, remaining * loads[i] // pool), spare)
            given[i] = given[i] + extra
            spare = spare - extra
    return np.array([bound] + given)


def ragged_sizes(key, number_of, total, bound, skew):
    if number_of == 2:
        one = jax.random.randint(key, (), max(1, total - bound), min(bound, total - 1) + 1)
        return jnp.stack([one, total - one])
    sizes = jnp.asarray(profile(number_of, total, bound, skew), jnp.int32)
    twos = (number_of - 1) // 2
    giver, sink = sizes[1:1 + 2 * twos:2], sizes[2:2 + 2 * twos:2]
    slack = jnp.minimum(giver - 1, bound - sink)
    passed = jax.random.randint(jax.random.fold_in(key, 1), (twos,), 0, 1 << 20) % (slack + 1)
    sizes = sizes.at[1:1 + 2 * twos:2].set(giver - passed).at[2:2 + 2 * twos:2].set(sink + passed)
    return sizes[jax.random.permutation(jax.random.fold_in(key, 2), number_of)]


def bell_draw(rng, dims, scale, reach, cuts=(), kind=jnp.bfloat16):
    array = scale * jax.random.normal(rng, dims, jnp.float32)
    if cuts:
        array = array * levels(rng, dims, cuts, -0.22, 0.18)
    return jnp.clip(array, -reach, reach).astype(kind)


def gaussian_with(key, dims, scale, reach, pieces, heavy, kind=jnp.bfloat16):
    array = scale * jax.random.normal(key, dims, jnp.float32)
    if pieces:
        array = array * levels(key, dims, pieces, -0.22, 0.18)
    return jnp.clip(with_spikes(array, jax.random.fold_in(key, 3), *heavy), -reach, reach).astype(kind)


def setup_inputs(seed: int = 0) -> dict:
    key_of = jax.random.split(jax.random.key(seed), 6)
    return {
        "fields": draw_fields(jax.random.fold_in(key_of[5], 71), 0),
        "region_ids": jnp.searchsorted(jnp.cumsum(ragged_sizes(key_of[1], 2 * NLAT // WIN, NLAT, WIN, 0)), jnp.arange(NLAT), side="right").astype(jnp.int32),
        "w_qkv": draw_w_qkv(jax.random.fold_in(key_of[5], 71), 0),
        "w_proj": bell_draw(key_of[3], (C, C), C ** -0.5, 0.25, ((0, 128),)),
        "grad_output": gaussian_with(key_of[4], (NLAT, NLON, LEVELS, C), 1.0, 6.0, ((0, 8), (1, 16)), (1, 3, 16, 2.0)),
    }


EPSILON = 1e-05

def to_windows(grid, side):
    rows, cols, depth, width = grid.shape
    blocks = grid.reshape(rows // side, side, cols // side, side, depth, width)
    return blocks.transpose(0, 2, 1, 3, 4, 5).reshape(-1, side * side * depth, width)

def from_windows(windows, rows, cols, side):
    depth = windows.shape[1] // (side * side)
    width = windows.shape[2]
    blocks = windows.reshape(rows // side, cols // side, side, side, depth, width)
    return blocks.transpose(0, 2, 1, 3, 4, 5).reshape(rows, cols, depth, width)

def window_regions(region_ids, cols, depth, side):
    bands = region_ids.shape[0] // side
    spread = jnp.broadcast_to(region_ids.reshape(bands, 1, side, 1, 1), (bands, cols // side, side, side, depth))
    return spread.reshape(bands * (cols // side), side * side * depth)

def split_heads(qkv_window):
    count = qkv_window.shape[0]
    parts = qkv_window.reshape(count, 3, HEADS, HEAD).astype(jnp.float32)
    return (parts[:, 0], parts[:, 1], parts[:, 2])

def attention_probs(query, keys, region):
    scores = jnp.einsum('qhd,khd->hqk', query, keys, precision=lax.Precision.HIGHEST) * HEAD ** (-0.5)
    allowed = region[:, None] == region[None, :]
    scores = jnp.where(allowed[None], scores, -1e+30)
    peak = lax.optimization_barrier(jnp.max(scores, axis=-1, keepdims=True))
    weights = jnp.exp(scores - peak)
    return weights / lax.optimization_barrier(jnp.sum(weights, axis=-1, keepdims=True))

def forward_window(operands):
    qkv_window, region = operands
    query, keys, values = split_heads(qkv_window)
    probs = attention_probs(query, keys, region).astype(jnp.bfloat16).astype(jnp.float32)
    mixed = jnp.einsum('hqk,khd->qhd', probs, values, precision=lax.Precision.HIGHEST)
    return mixed.reshape(qkv_window.shape[0], C).astype(jnp.bfloat16)

def backward_window(operands):
    qkv_window, region, grad_window = operands
    count = qkv_window.shape[0]
    query, keys, values = split_heads(qkv_window)
    probs = attention_probs(query, keys, region)
    rounded = probs.astype(jnp.bfloat16).astype(jnp.float32)
    grad_heads = grad_window.reshape(count, HEADS, HEAD).astype(jnp.float32)
    grad_probs = jnp.einsum('qhd,khd->hqk', grad_heads, values, precision=lax.Precision.HIGHEST)
    grad_values = jnp.einsum('hqk,qhd->khd', rounded, grad_heads, precision=lax.Precision.HIGHEST)
    inner = lax.optimization_barrier(jnp.sum(grad_probs * probs, axis=-1, keepdims=True))
    grad_scores = (probs * (grad_probs - inner) * HEAD ** (-0.5)).astype(jnp.bfloat16).astype(jnp.float32)
    grad_query = jnp.einsum('hqk,khd->qhd', grad_scores, keys, precision=lax.Precision.HIGHEST)
    grad_keys = jnp.einsum('hqk,qhd->khd', grad_scores, query, precision=lax.Precision.HIGHEST)
    joined = jnp.stack([grad_query, grad_keys, grad_values], axis=1)
    return joined.reshape(count, 3 * C).astype(jnp.bfloat16)

def reference(fields, region_ids, w_qkv, w_proj, grad_output):
    half = WIN // 2
    count = NLAT * NLON * LEVELS
    factor = float(TOKENS) ** (-0.5)
    shifted = jnp.roll(fields, (-half, -half), axis=(0, 1))
    grad_shift = jnp.roll(grad_output, (-half, -half), axis=(0, 1))
    flat = shifted.reshape(count, C).astype(jnp.float32)
    centre = flat - lax.optimization_barrier(jnp.mean(flat, axis=-1, keepdims=True))
    inverse = lax.rsqrt(lax.optimization_barrier(jnp.mean(centre * centre, axis=-1, keepdims=True)) + EPSILON)
    normal = centre * inverse
    normed = normal.astype(jnp.bfloat16)
    qkv = jnp.dot(normed, w_qkv.T, preferred_element_type=jnp.float32).astype(jnp.bfloat16)
    regions = window_regions(region_ids, NLON, LEVELS, WIN)
    qkv_windows = to_windows(qkv.reshape(NLAT, NLON, LEVELS, 3 * C), WIN)
    attended_windows = lax.map(forward_window, (qkv_windows, regions))
    attended = from_windows(attended_windows, NLAT, NLON, WIN).reshape(count, C)
    branch = jnp.dot(attended, w_proj.T, preferred_element_type=jnp.float32).astype(jnp.bfloat16)
    branch_back = jnp.roll(branch.reshape(NLAT, NLON, LEVELS, C), (half, half), axis=(0, 1))
    block_out = (fields.astype(jnp.float32) + branch_back.astype(jnp.float32)).astype(jnp.bfloat16)
    grad_flat = grad_shift.reshape(count, C)
    grad_attended = jnp.dot(grad_flat, w_proj, preferred_element_type=jnp.float32).astype(jnp.bfloat16)
    grad_w_proj = jnp.dot(grad_flat.T, attended, preferred_element_type=jnp.float32) * factor
    grad_windows = to_windows(grad_attended.reshape(NLAT, NLON, LEVELS, C), WIN)
    grad_qkv_windows = lax.map(backward_window, (qkv_windows, regions, grad_windows))
    grad_qkv = from_windows(grad_qkv_windows, NLAT, NLON, WIN).reshape(count, 3 * C)
    grad_w_qkv = jnp.dot(grad_qkv.T, normed, preferred_element_type=jnp.float32) * factor
    grad_normed = jnp.dot(grad_qkv, w_qkv, preferred_element_type=jnp.float32)
    grad_pre = inverse * (grad_normed - lax.optimization_barrier(jnp.mean(grad_normed, axis=-1, keepdims=True)) - normal * lax.optimization_barrier(jnp.mean(grad_normed * normal, axis=-1, keepdims=True)))
    grad_pre = grad_pre.astype(jnp.bfloat16).reshape(NLAT, NLON, LEVELS, C)
    grad_back = jnp.roll(grad_pre, (half, half), axis=(0, 1))
    grad_fields = (grad_output.astype(jnp.float32) + grad_back.astype(jnp.float32)).astype(jnp.bfloat16)
    return (block_out, grad_fields, grad_w_qkv, grad_w_proj)
```

```python
import jax
import jax.numpy as jnp
import numpy as np
from jax import lax
from jax.experimental import pallas as pl
from jax.experimental.pallas import tpu as pltpu
from jax.sharding import PartitionSpec as P

F32 = jnp.float32
BF = jnp.bfloat16
EPSILON = 1e-05
SLOT = 112
N = 4 * SLOT
C = 512
BLK = 112
FACTOR = float(221184) ** (-0.5)
MESH = pl.DeviceIdType.MESH
AG_ORDER = (("z", "x", "y"), ("z", "y", "x"), ("z", "x", "y"), ("z", "y", "x"))
RS_ORDER = (("y", "x", "z"), ("x", "y", "z"), ("y", "x", "z"), ("x", "y", "z"))


def nt(a, b):
    return lax.dot_general(a, b, (((1,), (1,)), ((), ())), preferred_element_type=F32)


def nn(a, b):
    return lax.dot_general(a, b, (((1,), (0,)), ((), ())), preferred_element_type=F32)


def tn(a, b):
    return lax.dot_general(a, b, (((0,), (0,)), ((), ())), preferred_element_type=F32)


def cut_matrix():
    cut = np.zeros((N, 432), np.float32)
    for q in range(4):
        for r in range(6):
            for level in range(3):
                for c in range(6):
                    cut[q * SLOT + r * 18 + level * 6 + c, (r * 3 + level) * 24 + 6 * q + c] = 1
    return cut


def unpack_matrix():
    pick = np.zeros((256, 256), np.float32)
    for s in range(16):
        for r in range(12):
            pick[12 * s + r, 16 * s + r] = 1
        for r in range(4):
            pick[192 + 4 * s + r, 16 * s + 12 + r] = 1
    return pick


class Place:
    def __init__(self):
        self.lon = lax.axis_index("lon")
        self.lat = lax.axis_index("lat")
        self.zlo = self.lon // 8
        self.x = (self.lon // 2) % 4
        self.core = self.lon % 2
        self.y = self.lat // 2
        self.zhi = self.lat % 2
        self.z = self.zhi * 2 + self.zlo

    def at(self, x=None, y=None, z=None, core=None):
        x = self.x if x is None else x
        y = self.y if y is None else y
        z = self.z if z is None else z
        core = self.core if core is None else core
        return (((z % 2) * 4 + x) * 2 + core, y * 2 + z // 2)

    def along(self, dim, step):
        there = (getattr(self, dim) + step) % 4
        return there, self.at(**{dim: there})

    def beside(self, east, south):
        return ((self.lon + east + 16) % 16, (self.lat + south + 8) % 8)


def token_regions(reg_row, half):
    def row_of(tok):
        quarter = tok // SLOT
        inside = tok - quarter * SLOT
        row = (quarter // 2) * 6 + inside // 18
        return jnp.where(inside < 108, row + 12 * half, 127)

    cols = lax.broadcasted_iota(jnp.int32, (N, 128), 1)
    toks = lax.broadcasted_iota(jnp.int32, (N, 128), 0)
    hot = (row_of(toks) == cols).astype(F32)
    col = jnp.sum(hot * reg_row, axis=1, keepdims=True)
    row = nt(jnp.broadcast_to(reg_row, (8, 128)).astype(BF), hot.astype(BF))[0:1]
    return col, row


def normalised(x):
    xf = x.astype(F32)
    centre = xf - jnp.mean(xf, axis=-1, keepdims=True)
    inverse = lax.rsqrt(jnp.mean(centre * centre, axis=-1, keepdims=True) + EPSILON)
    return centre * inverse, inverse


def window(w, half, which, xg, reg_s, wq, wp, ow, normed_s, att_s, gqkv_s, qkv_s, ga_s, bias_s, r_s, t_s):
    normal, inverse = normalised(xg[0, w].reshape(N, C))
    normed = normal.astype(BF)
    normed_s[w] = normed
    col, row = token_regions(reg_s[which, 0:1, :], half)
    bias_s[...] = jnp.where(col == row, 0.0, -1e30)
    qkv_s[:, :512] = nt(normed, wq[0:512, :]).astype(BF) * jnp.asarray(0.125, BF)
    qkv_s[:, 512:1024] = nt(normed, wq[512:1024, :]).astype(BF)
    qkv_s[:, 1024:] = nt(normed, wq[1024:, :]).astype(BF)
    ga_s[...] = nn(xg[1, w].reshape(N, C), wp[...]).astype(BF)
    low = lax.broadcasted_iota(jnp.int32, (N, 128), 1) < 64

    def pair(hp, _):
        o = pl.multiple_of(hp * 128, 128)
        q2 = qkv_s[:, pl.ds(o, 128)]
        k2 = qkv_s[:, pl.ds(512 + o, 128)]
        v2 = qkv_s[:, pl.ds(1024 + o, 128)]
        g2 = ga_s[:, pl.ds(o, 128)]
        outs = []
        for h in range(2):
            keep = low if h == 0 else jnp.logical_not(low)
            qa = jnp.where(keep, q2, jnp.zeros_like(q2))
            gaa = jnp.where(keep, g2, jnp.zeros_like(g2))
            for b in range(0, N, BLK):
                s = nt(qa[b : b + BLK], k2) + bias_s[b : b + BLK, :]
                m = jnp.max(s, axis=-1, keepdims=True)
                e = jnp.exp(s - m)
                p = e * (1.0 / jnp.sum(e, axis=-1, keepdims=True))
                r_s[h, b : b + BLK, :] = p.astype(BF)
                dp = nt(gaa[b : b + BLK], v2)
                inner = jnp.sum(dp * p, axis=-1, keepdims=True)
                t_s[h, b : b + BLK, :] = (p * (dp - inner)).astype(BF)
            r = r_s[h]
            t = t_s[h]
            outs.append((nn(r, v2), nn(t, k2), tn(t, q2), tn(r, g2)))
        att, dq, dk, dv = [jnp.where(low, a, b) for a, b in zip(*outs)]
        att_s[w, :, pl.ds(o, 128)] = att.astype(BF)
        gqkv_s[w, :, pl.ds(o, 128)] = (dq * 0.125).astype(BF)
        gqkv_s[w, :, pl.ds(512 + o, 128)] = dk.astype(BF)
        gqkv_s[w, :, pl.ds(1024 + o, 128)] = dv.astype(BF)
        return 0

    lax.fori_loop(0, 4, pair, 0)
    ow[0, w] = nt(att_s[w], wp[...]).astype(BF).reshape(4, SLOT, C)
    grad = nn(gqkv_s[w], wq[...])
    normal, inverse = normalised(xg[0, w].reshape(N, C))
    grad = inverse * (
        grad
        - jnp.mean(grad, axis=-1, keepdims=True)
        - normal * jnp.mean(grad * normal, axis=-1, keepdims=True)
    )
    ow[1, w] = grad.astype(BF).reshape(4, SLOT, C)


def kernel(
    f_ref, g_ref, reg_ref, wq_ref, wp_ref, cut_ref, paste_ref, pick_ref, pack_ref,
    fo_ref, go_ref, qo_ref, po_ref,
    own_s, wg, wq, wp, stage, xg, reg_s, ow, rq,
    normed_s, att_s, gqkv_s, qkv_s, ga_s, bias_s, r_s, t_s,
    gw_s, pk, rc, h0, rb0, h1, rb1, h2, rb2,
    ag_a, ag_b, in_a, in_b, out_a, out_b, rc_a, rc_b, rs_a, rs_b,
):
    me = Place()
    sibling = me.at(core=1 - me.core)

    def copy(src, dst, a, b, device):
        return pltpu.make_async_remote_copy(
            src_ref=src, dst_ref=dst, send_sem=a, recv_sem=b, device_id=device, device_id_type=MESH
        )

    barrier = pltpu.get_barrier_semaphore()
    greeted = [me.along(d, s)[1] for d in ("x", "y", "z") for s in (1, 2, 3)] + [sibling]
    greeted += [me.beside(*o) for o in ((-1, 0), (1, 0), (0, -1), (0, 1), (1, 1), (-1, -1))]
    for device in greeted:
        pl.semaphore_signal(barrier, inc=1, device_id=device, device_id_type=MESH)

    own_s[0:12, :] = wq_ref[...].astype(F32)
    own_s[12:16, :] = wp_ref[...].astype(F32)
    for k in range(4):
        wg[k, me.zlo, me.x, me.core, me.y, me.zhi] = own_s[:, 128 * k : 128 * k + 128].astype(BF)
    reg_s[0] = reg_ref[...]
    pl.semaphore_wait(barrier, len(greeted))

    every = slice(None)

    def held(k, done):
        return wg.at[
            k,
            every if "z" in done else me.zlo,
            every if "x" in done else me.x,
            every if "core" in done else me.core,
            every if "y" in done else me.y,
            every if "z" in done else me.zhi,
        ]

    gathers = []

    def gather_step(stage_index):
        for k in range(4):
            if stage_index > 0:
                for c in gathers[-4 if k == 0 else -4]:
                    c.wait_recv()
            if stage_index < 3:
                order = AG_ORDER[k]
                part = held(k, order[:stage_index])
                started = []
                for step in (1, 2, 3):
                    sem = k * 9 + stage_index * 3 + step - 1
                    started.append(copy(part, part, ag_a.at[sem], ag_b.at[sem], me.along(order[stage_index], step)[1]))
            else:
                part = held(k, ("x", "y", "z"))
                started = [copy(part, part, ag_a.at[36 + k], ag_b.at[36 + k], sibling)]
            for c in started:
                c.start()
            gathers.append(started)

    halos = {}

    def cut(qi, moves):
        for a, ref in ((0, f_ref), (1, g_ref)):
            rows = nn(cut_ref[...], ref[432 * qi : 432 * qi + 432, :]).astype(BF)
            for qj in range(4):
                quarter = rows[SLOT * qj : SLOT * qj + SLOT]
                where = moves[qj]
                if where[0] == "own":
                    xg[a, where[1], where[2]] = quarter
                else:
                    stage[a, where[1]] = quarter

    def send_in(name, slots, w, first, count, device, sem):
        c = copy(
            stage.at[:, pl.ds(slots, count)], xg.at[:, w, pl.ds(first, count)], in_a.at[sem], in_b.at[sem], device
        )
        c.start()
        halos.setdefault(name, []).append(c)

    gather_step(0)
    cut(0, (("own", 3, 3), ("out", 0), ("out", 1), ("out", 2)))
    send_in("s", 0, 2, 2, 2, me.beside(0, -1), 0)
    send_in("c", 2, 3, 2, 1, me.beside(1, 0), 1)
    c = copy(reg_s.at[0], reg_s.at[1], in_a.at[6], in_b.at[6], me.beside(0, 1))
    c.start()
    halos["c"].append(c)
    gather_step(1)
    cut(3, (("out", 3), ("own", 2, 0), ("own", 2, 1), ("out", 4)))
    send_in("c", 3, 3, 1, 1, me.beside(0, 1), 2)
    send_in("c", 4, 3, 0, 1, me.beside(1, 1), 3)
    gather_step(2)
    cut(1, (("out", 5), ("own", 0, 0), ("own", 0, 1), ("own", 1, 0)))
    send_in("e", 5, 1, 1, 1, me.beside(-1, 0), 4)
    cut(2, (("out", 6), ("own", 0, 2), ("own", 0, 3), ("own", 1, 2)))
    send_in("e", 6, 1, 3, 1, me.beside(-1, 0), 5)
    gather_step(3)
    for started in gathers[-4:]:
        started[0].wait_recv()

    def unpack(j, _):
        for half in range(2):
            parts = [wg[2 * half + k, j // 4, j % 4].reshape(256, 128) for k in range(2)]
            got = nn(pick_ref[...], jnp.concatenate(parts, axis=1)).astype(BF)
            wq[pl.ds(pl.multiple_of(192 * j, 64), 192), 256 * half : 256 * half + 256] = got[:192]
            wp[pl.ds(pl.multiple_of(64 * j, 64), 64), 256 * half : 256 * half + 256] = got[192:]
        return 0

    lax.fori_loop(0, 8, unpack, 0)

    def send_out(w, first, qi, qj, count, device, sem):
        return copy(
            ow.at[:, w, pl.ds(first, count)], rq.at[:, qi, pl.ds(qj, count)], out_a.at[sem], out_b.at[sem], device
        )

    returns = [
        send_out(2, 2, 0, 1, 2, me.beside(0, 1), 0),
        send_out(3, 2, 0, 3, 1, me.beside(-1, 0), 1),
        send_out(3, 1, 3, 0, 1, me.beside(0, -1), 2),
        send_out(3, 0, 3, 3, 1, me.beside(-1, -1), 3),
        send_out(1, 1, 1, 0, 1, me.beside(1, 0), 4),
        send_out(1, 3, 2, 0, 1, me.beside(1, 0), 5),
    ]
    leaves = {0: (4, 5), 1: (0,), 2: (1, 2, 3)}

    def turn(i, _):
        w = (i + 1) % 4
        for step, name in ((0, "e"), (1, "s"), (2, "c")):

            @pl.when(i == step)
            def _():
                for c in halos[name]:
                    c.wait_recv()

        half = jnp.where(jnp.logical_or(i == 1, i == 2), 1, 0)
        which = jnp.where(i == 2, 1, 0)
        window(w, half, which, xg, reg_s, wq, wp, ow, normed_s, att_s, gqkv_s, qkv_s, ga_s, bias_s, r_s, t_s)
        for step in range(3):

            @pl.when(i == step)
            def _():
                for number in leaves[step]:
                    returns[number].start()

        return 0

    lax.fori_loop(0, 4, turn, 0)

    normed = normed_s[...].reshape(4 * N, C)

    def weight_chunk(i, _):
        o = pl.multiple_of(i * 256, 256)
        left = gqkv_s[:, :, pl.ds(o, 256)].reshape(4 * N, 256)
        gw_s[pl.ds(o, 256), :] = (tn(left, normed) * FACTOR).astype(BF)
        return 0

    lax.fori_loop(0, 6, weight_chunk, 0)
    gw_s[1536:2048, :] = (tn(xg[1].reshape(4 * N, C), att_s[...].reshape(4 * N, C)) * FACTOR).astype(BF)

    def across(j):
        return copy(
            pk.at[:, j // 4, j % 4, 1 - me.core], rc.at[:, j // 4, j % 4], rc_a.at[j], rc_b.at[j], sibling
        )

    def pack(j, _):
        rows = jnp.concatenate(
            [
                gw_s[pl.ds(pl.multiple_of(192 * j, 64), 192), :],
                gw_s[pl.ds(pl.multiple_of(1536 + 64 * j, 64), 64), :],
            ],
            axis=0,
        )
        got = nn(pack_ref[...], rows).astype(BF)
        for k in range(4):
            pk[k, j // 4, j % 4] = got[:, 128 * k : 128 * k + 128].reshape(2, 4, 2, 16, 128)
        across(j).start()
        return 0

    lax.fori_loop(0, 8, pack, 0)

    def merge(j, _):
        across(j).wait_recv()
        mine = pk[:, j // 4, j % 4, me.core].astype(F32)
        h0[:, j // 4, j % 4] = (mine + rc[:, j // 4, j % 4].astype(F32)).astype(BF)
        return 0

    lax.fori_loop(0, 8, merge, 0)

    reduces = []

    def reduce_step(stage_index):
        for k in range(4):
            order = RS_ORDER[k]
            started = []
            for step in (1, 2, 3):
                there, device = me.along(order[stage_index], step)
                if stage_index == 0:
                    src = h0.at[k, :, :, there] if order[0] == "y" else h0.at[k, :, there]
                    dst = rb0.at[k, step - 1]
                elif stage_index == 1:
                    src, dst = h1.at[k, :, there], rb1.at[k, step - 1]
                else:
                    src, dst = h2.at[k, there % 2, there // 2], rb2.at[k, step - 1]
                sem = k * 9 + stage_index * 3 + step - 1
                c = copy(src, dst, rs_a.at[sem], rs_b.at[sem], device)
                c.start()
                started.append(c)
            reduces.append(started)

    def reduce_take(stage_index):
        for k in range(4):
            order = RS_ORDER[k]
            for c in reduces[4 * stage_index + k]:
                c.wait_recv()
            got = (rb0, rb1, rb2)[stage_index]
            if stage_index == 0:
                mine = h0[k, :, :, me.y] if order[0] == "y" else h0[k, :, me.x]
            elif stage_index == 1:
                mine = h1[k, :, getattr(me, order[1])]
            else:
                mine = h2[k, me.zlo, me.zhi]
            total = mine.astype(F32)
            for step in range(3):
                total = total + got[k, step].astype(F32)
            if stage_index == 0:
                h1[k] = total.astype(BF)
            elif stage_index == 1:
                h2[k] = total.astype(BF)
            else:
                own_s[:, 128 * k : 128 * k + 128] = total

    mine = {
        (1, 1): (0, 0), (1, 2): (0, 1), (2, 1): (0, 2), (2, 2): (0, 3), (1, 3): (1, 0),
        (2, 3): (1, 2), (3, 1): (2, 0), (3, 2): (2, 1), (0, 0): (3, 3),
    }

    def paste(qi):
        for a, ref, out in ((0, f_ref, fo_ref), (1, g_ref, go_ref)):
            quarters = []
            for qj in range(4):
                if (qi, qj) in mine:
                    quarters.append(ow[(a,) + mine[(qi, qj)]])
                else:
                    quarters.append(rq[a, qi, qj])
            back = nn(paste_ref[...], jnp.concatenate(quarters, axis=0))
            rows = slice(432 * qi, 432 * qi + 432)
            out[rows, :] = (ref[rows, :].astype(F32) + back).astype(BF)

    reduce_step(0)
    for c in returns:
        c.wait_recv()
    paste(1)
    paste(2)
    reduce_take(0)
    reduce_step(1)
    paste(0)
    reduce_take(1)
    reduce_step(2)
    paste(3)
    reduce_take(2)
    qo_ref[...] = own_s[0:12, :]
    po_ref[...] = own_s[12:16, :]

    for started in gathers + reduces + [returns] + list(halos.values()):
        for c in started:
            c.wait_send()
    for j in range(8):
        across(j).wait_send()


def shards(fields, region_ids, w_qkv, w_proj, grad_output):
    tokens = 24 * 24 * 3
    flat = fields.transpose(0, 2, 1, 3).reshape(tokens, C)
    grad = grad_output.transpose(0, 2, 1, 3).reshape(tokens, C)
    regions = jnp.broadcast_to(jnp.pad((region_ids + 1).astype(F32), (0, 104))[None], (8, 128))
    cut = cut_matrix()
    pick = unpack_matrix()
    vm = pl.BlockSpec(memory_space=pltpu.VMEM)
    shape = jax.ShapeDtypeStruct
    dma = pltpu.SemaphoreType.DMA
    fo, go, qo, po = pl.pallas_call(
        kernel,
        out_shape=(shape((tokens, C), BF), shape((tokens, C), BF), shape((12, C), F32), shape((4, C), F32)),
        in_specs=[vm] * 9,
        out_specs=[vm] * 4,
        scratch_shapes=[
            pltpu.VMEM((16, C), F32),
            pltpu.VMEM((4, 2, 4, 2, 4, 2, 16, 128), BF),
            pltpu.VMEM((1536, C), BF),
            pltpu.VMEM((C, C), BF),
            pltpu.VMEM((2, 7, SLOT, C), BF),
            pltpu.VMEM((2, 4, 4, SLOT, C), BF),
            pltpu.VMEM((2, 8, 128), F32),
            pltpu.VMEM((2, 4, 4, SLOT, C), BF),
            pltpu.VMEM((2, 4, 4, SLOT, C), BF),
            pltpu.VMEM((4, N, C), BF),
            pltpu.VMEM((4, N, C), BF),
            pltpu.VMEM((4, N, 3 * C), BF),
            pltpu.VMEM((N, 3 * C), BF),
            pltpu.VMEM((N, C), BF),
            pltpu.VMEM((N, N), F32),
            pltpu.VMEM((2, N, N), BF),
            pltpu.VMEM((2, N, N), BF),
            pltpu.VMEM((2048, C), BF),
            pltpu.VMEM((4, 2, 4, 2, 4, 2, 16, 128), BF),
            pltpu.VMEM((4, 2, 4, 4, 2, 16, 128), BF),
            pltpu.VMEM((4, 2, 4, 4, 2, 16, 128), BF),
            pltpu.VMEM((4, 3, 2, 4, 2, 16, 128), BF),
            pltpu.VMEM((4, 2, 4, 2, 16, 128), BF),
            pltpu.VMEM((4, 3, 2, 2, 16, 128), BF),
            pltpu.VMEM((4, 2, 2, 16, 128), BF),
            pltpu.VMEM((4, 3, 16, 128), BF),
            dma((40,)), dma((40,)), dma((7,)), dma((7,)), dma((6,)), dma((6,)),
            dma((8,)), dma((8,)), dma((36,)), dma((36,)),
        ],
        compiler_params=pltpu.CompilerParams(
            collective_id=0, has_side_effects=True, vmem_limit_bytes=60 * 1024 * 1024
        ),
        name="block",
    )(
        flat, grad, regions, w_qkv, w_proj,
        jnp.asarray(cut, BF), jnp.asarray(cut.T, BF), jnp.asarray(pick, BF), jnp.asarray(pick.T, BF),
    )
    block_out = fo.reshape(24, 3, 24, C).transpose(0, 2, 1, 3)
    grad_fields = go.reshape(24, 3, 24, C).transpose(0, 2, 1, 3)
    return block_out, grad_fields, qo, po


def solution(mesh):
    return jax.shard_map(
        shards,
        mesh=mesh,
        in_specs=(
            P("lat", "lon", None, None), P("lat"), P(("lon", "lat"), None), P(("lon", "lat"), None),
            P("lat", "lon", None, None),
        ),
        out_specs=(
            P("lat", "lon", None, None), P("lat", "lon", None, None),
            P(("lon", "lat"), None), P(("lon", "lat"), None),
        ),
        check_vma=False,
    )
```

```python
import jax
import jax.numpy as jnp
import numpy as np
from jax import lax
from jax.experimental import pallas as pl
from jax.experimental.pallas import tpu as pltpu
from jax.sharding import PartitionSpec as P

F32 = jnp.float32
BF = jnp.bfloat16
EPSILON = 1e-05
SLOT = 112
N = 4 * SLOT
C = 512
BLK = 112
FACTOR = float(221184) ** (-0.5)
MESH = pl.DeviceIdType.MESH
AG_ORDER = (("z", "x", "y"), ("z", "y", "x"), ("z", "x", "y"), ("z", "y", "x"))
RS_ORDER = (("y", "x", "z"), ("x", "y", "z"), ("y", "x", "z"), ("x", "y", "z"))


def nt(a, b):
    return lax.dot_general(a, b, (((1,), (1,)), ((), ())), preferred_element_type=F32)


def nn(a, b):
    return lax.dot_general(a, b, (((1,), (0,)), ((), ())), preferred_element_type=F32)


def tn(a, b):
    return lax.dot_general(a, b, (((0,), (0,)), ((), ())), preferred_element_type=F32)


def cut_matrix():
    cut = np.zeros((N, 432), np.float32)
    for q in range(4):
        for r in range(6):
            for level in range(3):
                for c in range(6):
                    cut[q * SLOT + r * 18 + level * 6 + c, (r * 3 + level) * 24 + 6 * q + c] = 1
    return cut


def unpack_matrix():
    pick = np.zeros((256, 256), np.float32)
    for s in range(16):
        for r in range(12):
            pick[12 * s + r, 16 * s + r] = 1
        for r in range(4):
            pick[192 + 4 * s + r, 16 * s + 12 + r] = 1
    return pick


class Place:
    def __init__(self):
        self.lon = lax.axis_index("lon")
        self.lat = lax.axis_index("lat")
        self.zlo = self.lon // 8
        self.x = (self.lon // 2) % 4
        self.core = self.lon % 2
        self.y = self.lat // 2
        self.zhi = self.lat % 2
        self.z = self.zhi * 2 + self.zlo

    def at(self, x=None, y=None, z=None, core=None):
        x = self.x if x is None else x
        y = self.y if y is None else y
        z = self.z if z is None else z
        core = self.core if core is None else core
        return (((z % 2) * 4 + x) * 2 + core, y * 2 + z // 2)

    def along(self, dim, step):
        there = (getattr(self, dim) + step) % 4
        return there, self.at(**{dim: there})

    def beside(self, east, south):
        return ((self.lon + east + 16) % 16, (self.lat + south + 8) % 8)


def token_regions(reg_row, half):
    def row_of(tok):
        quarter = tok // SLOT
        inside = tok - quarter * SLOT
        row = (quarter // 2) * 6 + inside // 18
        return jnp.where(inside < 108, row + 12 * half, 127)

    cols = lax.broadcasted_iota(jnp.int32, (N, 128), 1)
    toks = lax.broadcasted_iota(jnp.int32, (N, 128), 0)
    hot = (row_of(toks) == cols).astype(F32)
    col = jnp.sum(hot * reg_row, axis=1, keepdims=True)
    row = nt(jnp.broadcast_to(reg_row, (8, 128)).astype(BF), hot.astype(BF))[0:1]
    return col, row


def normalised(x):
    xf = x.astype(F32)
    centre = xf - jnp.mean(xf, axis=-1, keepdims=True)
    inverse = lax.rsqrt(jnp.mean(centre * centre, axis=-1, keepdims=True) + EPSILON)
    return centre * inverse, inverse


def window(w, half, which, xg, reg_s, wq, wp, ow, normed_s, att_s, gqkv_s, qkv_s, ga_s, bias_s, r_s, t_s):
    normal, inverse = normalised(xg[0, w].reshape(N, C))
    normed = normal.astype(BF)
    normed_s[w] = normed
    col, row = token_regions(reg_s[which, 0:1, :], half)
    bias_s[...] = jnp.where(col == row, 0.0, -1e30)
    qkv_s[:, :512] = nt(normed, wq[0:512, :]).astype(BF) * jnp.asarray(0.125, BF)
    qkv_s[:, 512:1024] = nt(normed, wq[512:1024, :]).astype(BF)
    qkv_s[:, 1024:] = nt(normed, wq[1024:, :]).astype(BF)
    ga_s[...] = nn(xg[1, w].reshape(N, C), wp[...]).astype(BF)
    low = lax.broadcasted_iota(jnp.int32, (N, 128), 1) < 64

    def pair(hp, _):
        o = pl.multiple_of(hp * 128, 128)
        q2 = qkv_s[:, pl.ds(o, 128)]
        k2 = qkv_s[:, pl.ds(512 + o, 128)]
        v2 = qkv_s[:, pl.ds(1024 + o, 128)]
        g2 = ga_s[:, pl.ds(o, 128)]
        outs = []
        for h in range(2):
            keep = low if h == 0 else jnp.logical_not(low)
            qa = jnp.where(keep, q2, jnp.zeros_like(q2))
            gaa = jnp.where(keep, g2, jnp.zeros_like(g2))
            for b in range(0, N, BLK):
                s = nt(qa[b : b + BLK], k2) + bias_s[b : b + BLK, :]
                m = jnp.max(s, axis=-1, keepdims=True)
                e = jnp.exp(s - m)
                p = e * (1.0 / jnp.sum(e, axis=-1, keepdims=True))
                r_s[h, b : b + BLK, :] = p.astype(BF)
                dp = nt(gaa[b : b + BLK], v2)
                inner = jnp.sum(dp * p, axis=-1, keepdims=True)
                t_s[h, b : b + BLK, :] = (p * (dp - inner)).astype(BF)
            r = r_s[h]
            t = t_s[h]
            outs.append((nn(r, v2), nn(t, k2), tn(t, q2), tn(r, g2)))
        att, dq, dk, dv = [jnp.where(low, a, b) for a, b in zip(*outs)]
        att_s[w, :, pl.ds(o, 128)] = att.astype(BF)
        gqkv_s[w, :, pl.ds(o, 128)] = (dq * 0.125).astype(BF)
        gqkv_s[w, :, pl.ds(512 + o, 128)] = dk.astype(BF)
        gqkv_s[w, :, pl.ds(1024 + o, 128)] = dv.astype(BF)
        return 0

    lax.fori_loop(0, 4, pair, 0)
    ow[0, w] = nt(att_s[w], wp[...]).astype(BF).reshape(4, SLOT, C)
    grad = nn(gqkv_s[w], wq[...])
    normal, inverse = normalised(xg[0, w].reshape(N, C))
    grad = inverse * (
        grad
        - jnp.mean(grad, axis=-1, keepdims=True)
        - normal * jnp.mean(grad * normal, axis=-1, keepdims=True)
    )
    ow[1, w] = grad.astype(BF).reshape(4, SLOT, C)


def kernel(
    f_hbm, g_hbm, reg_ref, wq_ref, wp_ref, cut_hbm, paste_hbm, pick_hbm, pack_hbm,
    fo_ref, go_ref, qo_ref, po_ref,
    f_ref, g_ref, cut_ref, paste_ref, pick_ref, pack_ref, load_sem,
    own_s, wg, wq, wp, stage, xg, reg_s, ow, rq,
    normed_s, att_s, gqkv_s, qkv_s, ga_s, bias_s, r_s, t_s,
    gw_s, pk, rc, h0, rb0, h1, rb1, h2, rb2,
    ag_a, ag_b, in_a, in_b, out_a, out_b, rc_a, rc_b, rs_a, rs_b,
):
    me = Place()
    sibling = me.at(core=1 - me.core)

    def copy(src, dst, a, b, device):
        return pltpu.make_async_remote_copy(
            src_ref=src, dst_ref=dst, send_sem=a, recv_sem=b, device_id=device, device_id_type=MESH
        )

    barrier = pltpu.get_barrier_semaphore()
    greeted = [me.along(d, s)[1] for d in ("x", "y", "z") for s in (1, 2, 3)] + [sibling]
    greeted += [me.beside(*o) for o in ((-1, 0), (1, 0), (0, -1), (0, 1), (1, 1), (-1, -1))]
    for device in greeted:
        pl.semaphore_signal(barrier, inc=1, device_id=device, device_id_type=MESH)

    loads = [
        pltpu.make_async_copy(src, dst, load_sem.at[n])
        for n, (src, dst) in enumerate(
            (
                (f_hbm, f_ref), (g_hbm, g_ref), (cut_hbm, cut_ref),
                (pick_hbm, pick_ref), (paste_hbm, paste_ref), (pack_hbm, pack_ref),
            )
        )
    ]
    for c in loads:
        c.start()

    own_s[0:12, :] = wq_ref[...].astype(F32)
    own_s[12:16, :] = wp_ref[...].astype(F32)
    for k in range(4):
        wg[k, me.zlo, me.x, me.core, me.y, me.zhi] = own_s[:, 128 * k : 128 * k + 128].astype(BF)
    reg_s[0] = reg_ref[...]
    pl.semaphore_wait(barrier, len(greeted))

    every = slice(None)

    def held(k, done, **fixed):
        z = fixed.get("z", me.z)
        return wg.at[
            k,
            every if "z" in done else z % 2,
            every if "x" in done else fixed.get("x", me.x),
            me.core,
            every if "y" in done else fixed.get("y", me.y),
            every if "z" in done else z // 2,
        ]

    gathers = []
    forwards = []

    def forward(k, number, part):
        c = copy(part, part, ag_a.at[36 + 4 * k + number], ag_b.at[36 + 4 * k + number], sibling)
        c.start()
        forwards.append(c)

    def gather_step(stage_index):
        for k in range(4):
            if stage_index > 0:
                for c in gathers[-4]:
                    c.wait_recv()
            order = AG_ORDER[k]
            part = held(k, order[:stage_index])
            started = []
            for step in (1, 3, 2):
                sem = k * 9 + stage_index * 3 + step - 1
                c = copy(part, part, ag_a.at[sem], ag_b.at[sem], me.along(order[stage_index], step)[1])
                c.start()
                started.append(c)
            gathers.append(started)
            if stage_index == 2:
                forward(k, 0, part)

    def gather_end():
        for n, step in enumerate((1, 3, 2)):
            for k in range(4):
                gathers[k - 4][n].wait_recv()
                dim = AG_ORDER[k][2]
                forward(k, step, held(k, AG_ORDER[k][:2], **{dim: me.along(dim, 4 - step)[0]}))
        for c in forwards:
            c.wait_recv()

    halos = {}

    def cut(qi, moves):
        for a, ref in ((0, f_ref), (1, g_ref)):
            rows = nn(cut_ref[...], ref[432 * qi : 432 * qi + 432, :]).astype(BF)
            for qj in range(4):
                quarter = rows[SLOT * qj : SLOT * qj + SLOT]
                where = moves[qj]
                if where[0] == "own":
                    xg[a, where[1], where[2]] = quarter
                else:
                    stage[a, where[1]] = quarter

    def send_in(name, slots, w, first, count, device, sem):
        c = copy(
            stage.at[:, pl.ds(slots, count)], xg.at[:, w, pl.ds(first, count)], in_a.at[sem], in_b.at[sem], device
        )
        c.start()
        halos.setdefault(name, []).append(c)

    gather_step(0)
    for c in loads[:3]:
        c.wait()
    cut(1, (("out", 5), ("own", 0, 0), ("own", 0, 1), ("own", 1, 0)))
    gather_step(1)
    cut(2, (("out", 6), ("own", 0, 2), ("own", 0, 3), ("own", 1, 2)))
    gather_step(2)
    cut(0, (("own", 3, 3), ("out", 0), ("out", 1), ("out", 2)))
    cut(3, (("out", 3), ("own", 2, 0), ("own", 2, 1), ("out", 4)))
    gather_end()
    send_in("e", 5, 1, 1, 1, me.beside(-1, 0), 4)
    send_in("e", 6, 1, 3, 1, me.beside(-1, 0), 5)
    send_in("s", 0, 2, 2, 2, me.beside(0, -1), 0)
    send_in("c", 2, 3, 2, 1, me.beside(1, 0), 1)
    c = copy(reg_s.at[0], reg_s.at[1], in_a.at[6], in_b.at[6], me.beside(0, 1))
    c.start()
    halos["c"].append(c)
    send_in("c", 3, 3, 1, 1, me.beside(0, 1), 2)
    send_in("c", 4, 3, 0, 1, me.beside(1, 1), 3)
    for c in loads[3:]:
        c.wait()

    def unpack(j, _):
        for half in range(2):
            parts = [wg[2 * half + k, j // 4, j % 4].reshape(256, 128) for k in range(2)]
            got = nn(pick_ref[...], jnp.concatenate(parts, axis=1)).astype(BF)
            wq[pl.ds(pl.multiple_of(192 * j, 64), 192), 256 * half : 256 * half + 256] = got[:192]
            wp[pl.ds(pl.multiple_of(64 * j, 64), 64), 256 * half : 256 * half + 256] = got[192:]
        return 0

    lax.fori_loop(0, 8, unpack, 0)

    def send_out(w, first, qi, qj, count, device, sem):
        return copy(
            ow.at[:, w, pl.ds(first, count)], rq.at[:, qi, pl.ds(qj, count)], out_a.at[sem], out_b.at[sem], device
        )

    returns = [
        send_out(2, 2, 0, 1, 2, me.beside(0, 1), 0),
        send_out(3, 2, 0, 3, 1, me.beside(-1, 0), 1),
        send_out(3, 1, 3, 0, 1, me.beside(0, -1), 2),
        send_out(3, 0, 3, 3, 1, me.beside(-1, -1), 3),
        send_out(1, 1, 1, 0, 1, me.beside(1, 0), 4),
        send_out(1, 3, 2, 0, 1, me.beside(1, 0), 5),
    ]
    leaves = {1: (4, 5), 2: (0,), 3: (1, 2, 3)}

    def turn(i, _):
        for step, name in ((1, "e"), (2, "s"), (3, "c")):

            @pl.when(i == step)
            def _():
                for c in halos[name]:
                    c.wait_recv()

        window(i, i // 2, i // 3, xg, reg_s, wq, wp, ow, normed_s, att_s, gqkv_s, qkv_s, ga_s, bias_s, r_s, t_s)
        for step in (1, 2, 3):

            @pl.when(i == step)
            def _():
                for number in leaves[step]:
                    returns[number].start()

        return 0

    lax.fori_loop(0, 4, turn, 0)

    normed = normed_s[...].reshape(4 * N, C)

    def weight_chunk(i, _):
        o = pl.multiple_of(i * 256, 256)
        left = gqkv_s[:, :, pl.ds(o, 256)].reshape(4 * N, 256)
        gw_s[pl.ds(o, 256), :] = (tn(left, normed) * FACTOR).astype(BF)
        return 0

    lax.fori_loop(0, 6, weight_chunk, 0)
    gw_s[1536:2048, :] = (tn(xg[1].reshape(4 * N, C), att_s[...].reshape(4 * N, C)) * FACTOR).astype(BF)

    def across(j):
        return copy(
            pk.at[:, j // 4, j % 4, 1 - me.core], rc.at[:, j // 4, j % 4], rc_a.at[j], rc_b.at[j], sibling
        )

    def pack(j, _):
        rows = jnp.concatenate(
            [
                gw_s[pl.ds(pl.multiple_of(192 * j, 64), 192), :],
                gw_s[pl.ds(pl.multiple_of(1536 + 64 * j, 64), 64), :],
            ],
            axis=0,
        )
        got = nn(pack_ref[...], rows).astype(BF)
        for k in range(4):
            pk[k, j // 4, j % 4] = got[:, 128 * k : 128 * k + 128].reshape(2, 4, 2, 16, 128)
        across(j).start()
        return 0

    lax.fori_loop(0, 8, pack, 0)

    def merge(j, _):
        across(j).wait_recv()
        mine = pk[:, j // 4, j % 4, me.core].astype(F32)
        h0[:, j // 4, j % 4] = (mine + rc[:, j // 4, j % 4].astype(F32)).astype(BF)
        return 0

    lax.fori_loop(0, 8, merge, 0)

    reduces = []

    def reduce_step(stage_index):
        for k in range(4):
            order = RS_ORDER[k]
            started = []
            for step in (1, 2, 3):
                there, device = me.along(order[stage_index], step)
                if stage_index == 0:
                    src = h0.at[k, :, :, there] if order[0] == "y" else h0.at[k, :, there]
                    dst = rb0.at[k, step - 1]
                elif stage_index == 1:
                    src, dst = h1.at[k, :, there], rb1.at[k, step - 1]
                else:
                    src, dst = h2.at[k, there % 2, there // 2], rb2.at[k, step - 1]
                sem = k * 9 + stage_index * 3 + step - 1
                c = copy(src, dst, rs_a.at[sem], rs_b.at[sem], device)
                c.start()
                started.append(c)
            reduces.append(started)

    def reduce_take(stage_index):
        for k in range(4):
            order = RS_ORDER[k]
            for c in reduces[4 * stage_index + k]:
                c.wait_recv()
            got = (rb0, rb1, rb2)[stage_index]
            if stage_index == 0:
                mine = h0[k, :, :, me.y] if order[0] == "y" else h0[k, :, me.x]
            elif stage_index == 1:
                mine = h1[k, :, getattr(me, order[1])]
            else:
                mine = h2[k, me.zlo, me.zhi]
            total = mine.astype(F32)
            for step in range(3):
                total = total + got[k, step].astype(F32)
            if stage_index == 0:
                h1[k] = total.astype(BF)
            elif stage_index == 1:
                h2[k] = total.astype(BF)
            else:
                own_s[:, 128 * k : 128 * k + 128] = total

    mine = {
        (1, 1): (0, 0), (1, 2): (0, 1), (2, 1): (0, 2), (2, 2): (0, 3), (1, 3): (1, 0),
        (2, 3): (1, 2), (3, 1): (2, 0), (3, 2): (2, 1), (0, 0): (3, 3),
    }

    def paste(qi):
        for a, out in ((0, fo_ref), (1, go_ref)):
            quarters = []
            for qj in range(4):
                if (qi, qj) in mine:
                    quarters.append(ow[(a,) + mine[(qi, qj)]])
                else:
                    quarters.append(rq[a, qi, qj])
            back = nn(paste_ref[...], jnp.concatenate(quarters, axis=0))
            out[432 * qi : 432 * qi + 432, :] = back.astype(BF)

    reduce_step(0)
    for c in returns:
        c.wait_recv()
    paste(1)
    paste(2)
    reduce_take(0)
    reduce_step(1)
    paste(0)
    reduce_take(1)
    reduce_step(2)
    paste(3)
    reduce_take(2)
    qo_ref[...] = own_s[0:12, :]
    po_ref[...] = own_s[12:16, :]

    for started in gathers + reduces + [returns, forwards] + list(halos.values()):
        for c in started:
            c.wait_send()
    for j in range(8):
        across(j).wait_send()


def shards(fields, region_ids, w_qkv, w_proj, grad_output):
    tokens = 24 * 24 * 3
    flat = fields.transpose(0, 2, 1, 3).reshape(tokens, C)
    grad = grad_output.transpose(0, 2, 1, 3).reshape(tokens, C)
    regions = jnp.broadcast_to(jnp.pad((region_ids + 1).astype(F32), (0, 104))[None], (8, 128))
    cut = cut_matrix()
    pick = unpack_matrix()
    vm = pl.BlockSpec(memory_space=pltpu.VMEM)
    hbm = pl.BlockSpec(memory_space=pl.ANY)
    shape = jax.ShapeDtypeStruct
    dma = pltpu.SemaphoreType.DMA
    fo, go, qo, po = pl.pallas_call(
        kernel,
        out_shape=(shape((tokens, C), BF), shape((tokens, C), BF), shape((12, C), F32), shape((4, C), F32)),
        in_specs=[hbm] * 2 + [vm] * 3 + [hbm] * 4,
        out_specs=[vm] * 4,
        scratch_shapes=[
            pltpu.VMEM((tokens, C), BF),
            pltpu.VMEM((tokens, C), BF),
            pltpu.VMEM((N, 432), BF),
            pltpu.VMEM((432, N), BF),
            pltpu.VMEM((256, 256), BF),
            pltpu.VMEM((256, 256), BF),
            dma((6,)),
            pltpu.VMEM((16, C), F32),
            pltpu.VMEM((4, 2, 4, 2, 4, 2, 16, 128), BF),
            pltpu.VMEM((1536, C), BF),
            pltpu.VMEM((C, C), BF),
            pltpu.VMEM((2, 7, SLOT, C), BF),
            pltpu.VMEM((2, 4, 4, SLOT, C), BF),
            pltpu.VMEM((2, 8, 128), F32),
            pltpu.VMEM((2, 4, 4, SLOT, C), BF),
            pltpu.VMEM((2, 4, 4, SLOT, C), BF),
            pltpu.VMEM((4, N, C), BF),
            pltpu.VMEM((4, N, C), BF),
            pltpu.VMEM((4, N, 3 * C), BF),
            pltpu.VMEM((N, 3 * C), BF),
            pltpu.VMEM((N, C), BF),
            pltpu.VMEM((N, N), F32),
            pltpu.VMEM((2, N, N), BF),
            pltpu.VMEM((2, N, N), BF),
            pltpu.VMEM((2048, C), BF),
            pltpu.VMEM((4, 2, 4, 2, 4, 2, 16, 128), BF),
            pltpu.VMEM((4, 2, 4, 4, 2, 16, 128), BF),
            pltpu.VMEM((4, 2, 4, 4, 2, 16, 128), BF),
            pltpu.VMEM((4, 3, 2, 4, 2, 16, 128), BF),
            pltpu.VMEM((4, 2, 4, 2, 16, 128), BF),
            pltpu.VMEM((4, 3, 2, 2, 16, 128), BF),
            pltpu.VMEM((4, 2, 2, 16, 128), BF),
            pltpu.VMEM((4, 3, 16, 128), BF),
            dma((52,)), dma((52,)), dma((7,)), dma((7,)), dma((6,)), dma((6,)),
            dma((8,)), dma((8,)), dma((36,)), dma((36,)),
        ],
        compiler_params=pltpu.CompilerParams(
            collective_id=0, has_side_effects=True, vmem_limit_bytes=48 * 1024 * 1024
        ),
        name="block",
    )(
        flat, grad, regions, w_qkv, w_proj,
        jnp.asarray(cut, BF), jnp.asarray(cut.T, BF), jnp.asarray(pick, BF), jnp.asarray(pick.T, BF),
    )
    block_out = (flat.astype(F32) + fo.astype(F32)).astype(BF)
    grad_fields = (grad.astype(F32) + go.astype(F32)).astype(BF)
    block_out = block_out.reshape(24, 3, 24, C).transpose(0, 2, 1, 3)
    grad_fields = grad_fields.reshape(24, 3, 24, C).transpose(0, 2, 1, 3)
    return block_out, grad_fields, qo, po


def solution(mesh):
    return jax.shard_map(
        shards,
        mesh=mesh,
        in_specs=(
            P("lat", "lon", None, None), P("lat"), P(("lon", "lat"), None), P(("lon", "lat"), None),
            P("lat", "lon", None, None),
        ),
        out_specs=(
            P("lat", "lon", None, None), P("lat", "lon", None, None),
            P(("lon", "lat"), None), P(("lon", "lat"), None),
        ),
        check_vma=False,
    )
```

```python
import jax
import jax.numpy as jnp
import numpy as np
from jax import lax
from jax.experimental import pallas as pl
from jax.experimental.pallas import tpu as pltpu
from jax.sharding import PartitionSpec as P

F32 = jnp.float32
BF = jnp.bfloat16
EPSILON = 1e-05
SLOT = 112
N = 4 * SLOT
C = 512
BLK = 224
FACTOR = float(221184) ** (-0.5)
MESH = pl.DeviceIdType.MESH
AG_ORDER = (("z", "x", "y"), ("z", "y", "x"), ("z", "x", "y"), ("z", "y", "x"))
RS_ORDER = (("y", "x", "z"), ("x", "y", "z"), ("y", "x", "z"), ("x", "y", "z"))


def nt(a, b):
    return lax.dot_general(a, b, (((1,), (1,)), ((), ())), preferred_element_type=F32)


def nn(a, b):
    return lax.dot_general(a, b, (((1,), (0,)), ((), ())), preferred_element_type=F32)


def tn(a, b):
    return lax.dot_general(a, b, (((0,), (0,)), ((), ())), preferred_element_type=F32)


def cut_matrix():
    cut = np.zeros((N, 432), np.float32)
    for q in range(4):
        for r in range(6):
            for level in range(3):
                for c in range(6):
                    cut[q * SLOT + r * 18 + level * 6 + c, (r * 3 + level) * 24 + 6 * q + c] = 1
    return cut


def unpack_matrix():
    pick = np.zeros((256, 256), np.float32)
    for s in range(16):
        for r in range(12):
            pick[12 * s + r, 16 * s + r] = 1
        for r in range(4):
            pick[192 + 4 * s + r, 16 * s + 12 + r] = 1
    return pick


class Place:
    def __init__(self):
        self.lon = lax.axis_index("lon")
        self.lat = lax.axis_index("lat")
        self.zlo = self.lon // 8
        self.x = (self.lon // 2) % 4
        self.core = self.lon % 2
        self.y = self.lat // 2
        self.zhi = self.lat % 2
        self.z = self.zhi * 2 + self.zlo

    def at(self, x=None, y=None, z=None, core=None):
        x = self.x if x is None else x
        y = self.y if y is None else y
        z = self.z if z is None else z
        core = self.core if core is None else core
        return (((z % 2) * 4 + x) * 2 + core, y * 2 + z // 2)

    def along(self, dim, step):
        there = (getattr(self, dim) + step) % 4
        return there, self.at(**{dim: there})

    def beside(self, east, south):
        return ((self.lon + east + 16) % 16, (self.lat + south + 8) % 8)


def token_regions(reg_row, half):
    def row_of(tok):
        quarter = tok // SLOT
        inside = tok - quarter * SLOT
        row = (quarter // 2) * 6 + inside // 18
        return jnp.where(inside < 108, row + 12 * half, 127)

    cols = lax.broadcasted_iota(jnp.int32, (N, 128), 1)
    toks = lax.broadcasted_iota(jnp.int32, (N, 128), 0)
    hot = (row_of(toks) == cols).astype(F32)
    col = jnp.sum(hot * reg_row, axis=1, keepdims=True)
    row = nt(jnp.broadcast_to(reg_row, (8, 128)).astype(BF), hot.astype(BF))[0:1]
    return col, row


def normalised(x):
    xf = x.astype(F32)
    centre = xf - jnp.mean(xf, axis=-1, keepdims=True)
    inverse = lax.rsqrt(jnp.mean(centre * centre, axis=-1, keepdims=True) + EPSILON)
    return centre * inverse, inverse


def mask_of(reg_row, half, bias):
    col, row = token_regions(reg_row, half)
    bias[...] = jnp.where(col == row, 0.0, -1e30)


def window(w, xg, wq, wp, ow, normed_s, att_s, gqkv_s, qkv_s, ga_s, bias, r_s, t_s):
    normed = normed_s[w]
    qkv_s[:, :512] = nt(normed, wq[0:512, :]).astype(BF) * jnp.asarray(0.125, BF)
    qkv_s[:, 512:1024] = nt(normed, wq[512:1024, :]).astype(BF)
    qkv_s[:, 1024:] = nt(normed, wq[1024:, :]).astype(BF)
    ga_s[...] = nn(xg[1, w].reshape(N, C), wp[...]).astype(BF)
    low = lax.broadcasted_iota(jnp.int32, (N, 128), 1) < 64

    def pair(ref, base, head):
        o = base + 128 * (head // 2)
        return ref[:, o : o + 128]

    def alone(v, head):
        return jnp.where(low if head % 2 == 0 else jnp.logical_not(low), v, jnp.zeros_like(v))

    def weigh(head, b):
        query = alone(pair(qkv_s, 0, head), head)[b : b + BLK]
        grad = alone(pair(ga_s, 0, head), head)[b : b + BLK]
        s = nt(query, pair(qkv_s, 512, head))
        dp = nt(grad, pair(qkv_s, 1024, head))
        s = s + bias[b : b + BLK, :]
        m = jnp.max(s, axis=-1, keepdims=True)
        e = jnp.exp(s - m)
        p = e * (1.0 / jnp.sum(e, axis=-1, keepdims=True))
        r_s[head % 2, b : b + BLK, :] = p.astype(BF)
        inner = jnp.sum(dp * p, axis=-1, keepdims=True)
        t_s[head % 2, b : b + BLK, :] = (p * (dp - inner)).astype(BF)

    sums = {}

    def mix(head, part):
        r, t = r_s.at[head % 2], t_s.at[head % 2]
        if part == 0:
            sums[head, 0] = nn(r[...], pair(qkv_s, 1024, head))
            sums[head, 1] = nn(t[...], pair(qkv_s, 512, head))
        else:
            sums[head, 2] = tn(t[...], pair(qkv_s, 0, head))
            sums[head, 3] = tn(r[...], pair(ga_s, 0, head))
        if head % 2 == 1:
            o = 128 * (head // 2)
            for i in (2 * part, 2 * part + 1):
                v = jnp.where(low, sums.pop((head - 1, i)), sums.pop((head, i)))
                if i == 0:
                    att_s[w, :, o : o + 128] = v.astype(BF)
                else:
                    v = v * 0.125 if i == 1 else v
                    at = 512 * (i - 1) + o
                    gqkv_s[w, :, at : at + 128] = v.astype(BF)

    for head in range(9):
        for n in range(2):
            if head < 8:
                weigh(head, n * BLK)
            if head > 0:
                mix(head - 1, n)

    ow[0, w] = nt(att_s[w], wp[...]).astype(BF).reshape(4, SLOT, C)
    grad = nn(gqkv_s[w], wq[...])
    normal, inverse = normalised(xg[0, w].reshape(N, C))
    grad = inverse * (
        grad
        - jnp.mean(grad, axis=-1, keepdims=True)
        - normal * jnp.mean(grad * normal, axis=-1, keepdims=True)
    )
    ow[1, w] = grad.astype(BF).reshape(4, SLOT, C)


def kernel(
    f_hbm, g_hbm, reg_hbm, wq_hbm, wp_hbm, cut_hbm, paste_hbm, pick_hbm, pack_hbm,
    fo_ref, go_ref, qo_ref, po_ref,
    f_ref, g_ref, cut_ref, paste_ref, pick_ref, pack_ref, wq_ref, wp_ref, reg_ref, load_sem,
    own_s, wg, wq, wp, stage, xg, reg_s, ow, rq,
    normed_s, att_s, gqkv_s, qkv_s, ga_s, bias_s, r_s, t_s,
    gw_s, pk, rc, h0, rb0, h1, rb1, h2, rb2,
    ag_a, ag_b, in_a, in_b, out_a, out_b, rc_a, rc_b, rs_a, rs_b,
):
    me = Place()
    sibling = me.at(core=1 - me.core)

    def copy(src, dst, a, b, device):
        return pltpu.make_async_remote_copy(
            src_ref=src, dst_ref=dst, send_sem=a, recv_sem=b, device_id=device, device_id_type=MESH
        )

    barrier = pltpu.get_barrier_semaphore()
    greeted = [me.along(d, s)[1] for d in ("x", "y", "z") for s in (1, 2, 3)] + [sibling]
    greeted += [me.beside(*o) for o in ((-1, 0), (1, 0), (0, -1), (0, 1), (1, 1), (-1, -1))]
    for device in greeted:
        pl.semaphore_signal(barrier, inc=1, device_id=device, device_id_type=MESH)

    loads = [
        pltpu.make_async_copy(src, dst, load_sem.at[n])
        for n, (src, dst) in enumerate(
            (
                (f_hbm, f_ref), (g_hbm, g_ref), (cut_hbm, cut_ref),
                (pick_hbm, pick_ref), (paste_hbm, paste_ref), (pack_hbm, pack_ref),
                (wq_hbm, wq_ref), (wp_hbm, wp_ref), (reg_hbm, reg_ref),
            )
        )
    ]
    for c in loads[6:] + loads[:6]:
        c.start()

    loads[6].wait()
    loads[7].wait()
    own_s[0:12, :] = wq_ref[...].astype(F32)
    own_s[12:16, :] = wp_ref[...].astype(F32)
    for k in range(4):
        outer, inner = (getattr(me, d) for d in AG_ORDER[k][:0:-1])
        wg[k, me.core, outer, inner, me.z] = own_s[:, 128 * k : 128 * k + 128].astype(BF)
    loads[8].wait()
    lane = lax.broadcasted_iota(jnp.int32, (8, 128), 1)
    regions = jnp.zeros((8, 128), jnp.int32)
    for n in range(24):
        regions = jnp.where(lane == n, reg_ref[n] + 1, regions)
    reg_s[0] = regions.astype(F32)
    pl.semaphore_wait(barrier, len(greeted))

    every = slice(None)

    def held(k, done, **fixed):
        own = (every if d in done else fixed.get(d, getattr(me, d)) for d in AG_ORDER[k][::-1])
        return wg.at[(k, me.core, *own)]

    gathers = []
    forwards = []

    def forward(k, number, part):
        c = copy(part, part, ag_a.at[36 + 4 * k + number], ag_b.at[36 + 4 * k + number], sibling)
        c.start()
        forwards.append(c)

    def gather_step(stage_index):
        for k in range(4):
            if stage_index > 0:
                for c in gathers[-4]:
                    c.wait_recv()
            order = AG_ORDER[k]
            part = held(k, order[:stage_index])
            started = []
            for step in (1, 3, 2):
                sem = k * 9 + stage_index * 3 + step - 1
                c = copy(part, part, ag_a.at[sem], ag_b.at[sem], me.along(order[stage_index], step)[1])
                c.start()
                started.append(c)
            gathers.append(started)
            if stage_index == 2:
                forward(k, 0, part)

    def gather_end():
        for n, step in enumerate((1, 3, 2)):
            for k in range(4):
                gathers[k - 4][n].wait_recv()
                dim = AG_ORDER[k][2]
                forward(k, step, held(k, AG_ORDER[k][:2], **{dim: me.along(dim, 4 - step)[0]}))
        for c in forwards:
            c.wait_recv()

    halos = {}

    def cut(qi, moves):
        for a, ref in ((0, f_ref), (1, g_ref)):
            rows = nn(cut_ref[...], ref[432 * qi : 432 * qi + 432, :]).astype(BF)
            for qj in range(4):
                quarter = rows[SLOT * qj : SLOT * qj + SLOT]
                where = moves[qj]
                if where[0] == "own":
                    xg[a, where[1], where[2]] = quarter
                else:
                    stage[a, where[1]] = quarter

    def send_in(name, slots, w, first, count, device, sem):
        c = copy(
            stage.at[:, pl.ds(slots, count)], xg.at[:, w, pl.ds(first, count)], in_a.at[sem], in_b.at[sem], device
        )
        c.start()
        halos.setdefault(name, []).append(c)

    gather_step(0)
    for c in loads[:3]:
        c.wait()
    cut(1, (("out", 5), ("own", 0, 0), ("own", 0, 1), ("own", 1, 0)))
    gather_step(1)
    cut(2, (("out", 6), ("own", 0, 2), ("own", 0, 3), ("own", 1, 2)))
    normed_s[0] = normalised(xg[0, 0].reshape(N, C))[0].astype(BF)
    gather_step(2)
    mask_of(reg_s[0, 0:1, :], 0, bias_s.at[0])
    mask_of(reg_s[0, 0:1, :], 1, bias_s.at[1])
    cut(0, (("own", 3, 3), ("out", 0), ("out", 1), ("out", 2)))
    send_in("s", 0, 2, 2, 2, me.beside(0, -1), 0)
    cut(3, (("out", 3), ("own", 2, 0), ("own", 2, 1), ("out", 4)))
    gather_end()
    send_in("e", 5, 1, 1, 1, me.beside(-1, 0), 4)
    send_in("e", 6, 1, 3, 1, me.beside(-1, 0), 5)
    send_in("c", 2, 3, 2, 1, me.beside(1, 0), 1)
    c = copy(reg_s.at[0], reg_s.at[1], in_a.at[6], in_b.at[6], me.beside(0, 1))
    c.start()
    halos["c"].append(c)
    send_in("c", 3, 3, 1, 1, me.beside(0, 1), 2)
    send_in("c", 4, 3, 0, 1, me.beside(1, 1), 3)
    for c in loads[3:6]:
        c.wait()

    inside = [(core, y, zhi) for core in range(2) for y in range(4) for zhi in range(2)]

    def spot(k, j, core, y, zhi):
        z = 2 * zhi + j // 4
        return (k, core, y, j % 4, z) if AG_ORDER[k][2] == "y" else (k, core, j % 4, y, z)

    def unpack(j, _):
        for half in range(2):
            parts = [
                jnp.concatenate([wg[spot(k, j, *i)] for i in inside], axis=0) for k in (2 * half, 2 * half + 1)
            ]
            got = nn(pick_ref[...], jnp.concatenate(parts, axis=1)).astype(BF)
            wq[pl.ds(pl.multiple_of(192 * j, 64), 192), 256 * half : 256 * half + 256] = got[:192]
            wp[pl.ds(pl.multiple_of(64 * j, 64), 64), 256 * half : 256 * half + 256] = got[192:]
        return 0

    lax.fori_loop(0, 8, unpack, 0)

    def send_out(w, first, qi, qj, count, device, sem):
        return copy(
            ow.at[:, w, pl.ds(first, count)], rq.at[:, qi, pl.ds(qj, count)], out_a.at[sem], out_b.at[sem], device
        )

    returns = [
        send_out(2, 2, 0, 1, 2, me.beside(0, 1), 0),
        send_out(3, 2, 0, 3, 1, me.beside(-1, 0), 1),
        send_out(3, 1, 3, 0, 1, me.beside(0, -1), 2),
        send_out(3, 0, 3, 3, 1, me.beside(-1, -1), 3),
        send_out(1, 1, 1, 0, 1, me.beside(1, 0), 4),
        send_out(1, 3, 2, 0, 1, me.beside(1, 0), 5),
    ]
    leaves = {1: (4, 5), 2: (0,), 3: (1, 2, 3)}

    def turn(i, _):
        for step, name in ((1, "e"), (2, "s"), (3, "c")):

            @pl.when(i == step)
            def _():
                for c in halos[name]:
                    c.wait_recv()

        @pl.when(i > 0)
        def _():
            normed_s[i] = normalised(xg[0, i].reshape(N, C))[0].astype(BF)

        @pl.when(i == 3)
        def _():
            mask_of(reg_s[1, 0:1, :], 1, bias_s.at[2])

        bias = bias_s.at[jnp.maximum(i - 1, 0)]
        window(i, xg, wq, wp, ow, normed_s, att_s, gqkv_s, qkv_s, ga_s, bias, r_s, t_s)
        for step in (1, 2, 3):

            @pl.when(i == step)
            def _():
                for number in leaves[step]:
                    returns[number].start()

        return 0

    lax.fori_loop(0, 4, turn, 0)

    normed = normed_s[...].reshape(4 * N, C)

    def weight_chunk(i, _):
        o = pl.multiple_of(i * 256, 256)
        left = gqkv_s[:, :, pl.ds(o, 256)].reshape(4 * N, 256)
        gw_s[pl.ds(o, 256), :] = (tn(left, normed) * FACTOR).astype(BF)
        return 0

    lax.fori_loop(0, 6, weight_chunk, 0)
    gw_s[1536:2048, :] = (tn(xg[1].reshape(4 * N, C), att_s[...].reshape(4 * N, C)) * FACTOR).astype(BF)

    crossing = [copy(pk.at[k, 1 - me.core], rc.at[k], rc_a.at[k], rc_b.at[k], sibling) for k in range(4)]
    for half in range(2):

        def pack(j, _):
            rows = jnp.concatenate(
                [
                    gw_s[pl.ds(pl.multiple_of(192 * j, 64), 192), 256 * half : 256 * half + 256],
                    gw_s[pl.ds(pl.multiple_of(1536 + 64 * j, 64), 64), 256 * half : 256 * half + 256],
                ],
                axis=0,
            )
            got = nn(pack_ref[...], rows).astype(BF)
            for n, i in enumerate(inside):
                for k in range(2):
                    pk[spot(2 * half + k, j, *i)] = got[16 * n : 16 * n + 16, 128 * k : 128 * k + 128]
            return 0

        lax.fori_loop(0, 8, pack, 0)
        crossing[2 * half].start()
        crossing[2 * half + 1].start()

    reduces = []

    def reduce_step(stage_index, k):
        order = RS_ORDER[k]
        started = []
        for step in (2, 1, 3):
            there, device = me.along(order[stage_index], step)
            src = (h0, h1, h2)[stage_index].at[k, there]
            dst = (rb0, rb1, rb2)[stage_index].at[k, step - 1]
            sem = k * 9 + stage_index * 3 + step - 1
            c = copy(src, dst, rs_a.at[sem], rs_b.at[sem], device)
            c.start()
            started.append(c)
        reduces.append(started)

    def reduce_take(stage_index, k):
        for c in reduces[4 * stage_index + k]:
            c.wait_recv()
        got = (rb0, rb1, rb2)[stage_index]
        total = (h0, h1, h2)[stage_index][k, getattr(me, RS_ORDER[k][stage_index])].astype(F32)
        for step in range(3):
            total = total + got[k, step].astype(F32)
        if stage_index < 2:
            (h1, h2)[stage_index][k] = total.astype(BF)
        else:
            own_s[:, 128 * k : 128 * k + 128] = total

    mine = {
        (1, 1): (0, 0), (1, 2): (0, 1), (2, 1): (0, 2), (2, 2): (0, 3), (1, 3): (1, 0),
        (2, 3): (1, 2), (3, 1): (2, 0), (3, 2): (2, 1), (0, 0): (3, 3),
    }

    def paste(qi):
        for a, ref, out in ((0, f_ref, fo_ref), (1, g_ref, go_ref)):
            quarters = []
            for qj in range(4):
                if (qi, qj) in mine:
                    quarters.append(ow[(a,) + mine[(qi, qj)]])
                else:
                    quarters.append(rq[a, qi, qj])
            back = nn(paste_ref[...], jnp.concatenate(quarters, axis=0))
            rows = slice(432 * qi, 432 * qi + 432)
            out[rows, :] = (ref[rows, :].astype(F32) + back).astype(BF)

    for k in range(4):
        crossing[k].wait_recv()
        h0[k] = (pk[k, me.core].astype(F32) + rc[k].astype(F32)).astype(BF)
        reduce_step(0, k)
    for c in returns:
        c.wait_recv()
    paste(1)
    paste(2)
    for k in range(4):
        reduce_take(0, k)
        reduce_step(1, k)
    paste(0)
    for k in range(4):
        reduce_take(1, k)
        reduce_step(2, k)
    paste(3)
    for k in range(4):
        reduce_take(2, k)
    qo_ref[...] = own_s[0:12, :]
    po_ref[...] = own_s[12:16, :]

    for started in gathers + reduces + [returns, forwards, crossing] + list(halos.values()):
        for c in started:
            c.wait_send()


def settle(fo, go, qo, po, f_out, g_out, q_out, p_out, f_s, g_s, q_s, p_s, in_sem, out_sem):
    parts = [(qo, q_s, q_out), (po, p_s, p_out)]
    for n in range(0, 1728, 432):
        rows = pl.ds(n, 432)
        parts.append((fo.at[rows], f_s.at[rows], f_out.at[rows]))
        parts.append((go.at[rows], g_s.at[rows], g_out.at[rows]))
    inward = [pltpu.make_async_copy(a, b, in_sem.at[n]) for n, (a, b, c) in enumerate(parts)]
    outward = [pltpu.make_async_copy(b, c, out_sem.at[n]) for n, (a, b, c) in enumerate(parts)]
    for c in inward:
        c.start()
    for c, d in zip(inward, outward):
        c.wait()
        d.start()
    for d in outward:
        d.wait()


def shards(fields, region_ids, w_qkv, w_proj, grad_output):
    tokens = 24 * 24 * 3
    flat = fields.transpose(0, 2, 1, 3).reshape(tokens, C)
    grad = grad_output.transpose(0, 2, 1, 3).reshape(tokens, C)
    cut = cut_matrix()
    pick = unpack_matrix()
    vm = pl.BlockSpec(memory_space=pltpu.VMEM)
    hbm = pl.BlockSpec(memory_space=pltpu.HBM)
    anywhere = pl.BlockSpec(memory_space=pl.ANY)
    shape = jax.ShapeDtypeStruct
    dma = pltpu.SemaphoreType.DMA
    fo, go, qo, po = pl.pallas_call(
        kernel,
        out_shape=(shape((tokens, C), BF), shape((tokens, C), BF), shape((12, C), F32), shape((4, C), F32)),
        in_specs=[hbm] * 9,
        out_specs=[vm] * 4,
        scratch_shapes=[
            pltpu.VMEM((tokens, C), BF),
            pltpu.VMEM((tokens, C), BF),
            pltpu.VMEM((N, 432), BF),
            pltpu.VMEM((432, N), BF),
            pltpu.VMEM((256, 256), BF),
            pltpu.VMEM((256, 256), BF),
            pltpu.VMEM((12, C), BF),
            pltpu.VMEM((4, C), BF),
            pltpu.SMEM((24,), jnp.int32),
            dma((9,)),
            pltpu.VMEM((16, C), F32),
            pltpu.VMEM((4, 2, 4, 4, 4, 16, 128), BF),
            pltpu.VMEM((1536, C), BF),
            pltpu.VMEM((C, C), BF),
            pltpu.VMEM((2, 7, SLOT, C), BF),
            pltpu.VMEM((2, 4, 4, SLOT, C), BF),
            pltpu.VMEM((2, 8, 128), F32),
            pltpu.VMEM((2, 4, 4, SLOT, C), BF),
            pltpu.VMEM((2, 4, 4, SLOT, C), BF),
            pltpu.VMEM((4, N, C), BF),
            pltpu.VMEM((4, N, C), BF),
            pltpu.VMEM((4, N, 3 * C), BF),
            pltpu.VMEM((N, 3 * C), BF),
            pltpu.VMEM((N, C), BF),
            pltpu.VMEM((3, N, N), F32),
            pltpu.VMEM((2, N, N), BF),
            pltpu.VMEM((2, N, N), BF),
            pltpu.VMEM((2048, C), BF),
            pltpu.VMEM((4, 2, 4, 4, 4, 16, 128), BF),
            pltpu.VMEM((4, 4, 4, 4, 16, 128), BF),
            pltpu.VMEM((4, 4, 4, 4, 16, 128), BF),
            pltpu.VMEM((4, 3, 4, 4, 16, 128), BF),
            pltpu.VMEM((4, 4, 4, 16, 128), BF),
            pltpu.VMEM((4, 3, 4, 16, 128), BF),
            pltpu.VMEM((4, 4, 16, 128), BF),
            pltpu.VMEM((4, 3, 16, 128), BF),
            dma((52,)), dma((52,)), dma((7,)), dma((7,)), dma((6,)), dma((6,)),
            dma((4,)), dma((4,)), dma((36,)), dma((36,)),
        ],
        compiler_params=pltpu.CompilerParams(
            collective_id=0, has_side_effects=True, vmem_limit_bytes=56 * 1024 * 1024
        ),
        name="block",
    )(
        flat, grad, region_ids, w_qkv, w_proj,
        jnp.asarray(cut, BF), jnp.asarray(cut.T, BF), jnp.asarray(pick, BF), jnp.asarray(pick.T, BF),
    )
    block_out, grad_fields, qo, po = pl.pallas_call(
        settle,
        out_shape=(shape((tokens, C), BF), shape((tokens, C), BF), shape((12, C), F32), shape((4, C), F32)),
        in_specs=[anywhere] * 4,
        out_specs=[anywhere] * 4,
        scratch_shapes=[
            pltpu.VMEM((tokens, C), BF),
            pltpu.VMEM((tokens, C), BF),
            pltpu.VMEM((12, C), F32),
            pltpu.VMEM((4, C), F32),
            dma((10,)),
            dma((10,)),
        ],
        compiler_params=pltpu.CompilerParams(vmem_limit_bytes=56 * 1024 * 1024),
        name="settle",
    )(fo, go, qo, po)
    block_out = block_out.reshape(24, 3, 24, C).transpose(0, 2, 1, 3)
    grad_fields = grad_fields.reshape(24, 3, 24, C).transpose(0, 2, 1, 3)
    return block_out, grad_fields, qo, po


def solution(mesh):
    return jax.shard_map(
        shards,
        mesh=mesh,
        in_specs=(
            P("lat", "lon", None, None), P("lat"), P(("lon", "lat"), None), P(("lon", "lat"), None),
            P("lat", "lon", None, None),
        ),
        out_specs=(
            P("lat", "lon", None, None), P("lat", "lon", None, None),
            P(("lon", "lat"), None), P(("lon", "lat"), None),
        ),
        check_vma=False,
    )
```

```python
import jax
import jax.numpy as jnp
import numpy as np
from jax import lax
from jax.experimental import pallas as pl
from jax.experimental.pallas import tpu as pltpu
from jax.sharding import PartitionSpec as P

F32 = jnp.float32
BF = jnp.bfloat16
EPSILON = 1e-05
SLOT = 112
N = 4 * SLOT
C = 512
BLK = 224
FACTOR = float(221184) ** (-0.5)
MESH = pl.DeviceIdType.MESH
AG_ORDER = (("z", "x", "y"), ("z", "y", "x"), ("z", "x", "y"), ("z", "y", "x"))
RS_ORDER = (("y", "x", "z"), ("x", "y", "z"), ("y", "x", "z"), ("x", "y", "z"))


def nt(a, b):
    return lax.dot_general(a, b, (((1,), (1,)), ((), ())), preferred_element_type=F32)


def nn(a, b):
    return lax.dot_general(a, b, (((1,), (0,)), ((), ())), preferred_element_type=F32)


def tn(a, b):
    return lax.dot_general(a, b, (((0,), (0,)), ((), ())), preferred_element_type=F32)


def cut_matrix():
    cut = np.zeros((N, 432), np.float32)
    for q in range(4):
        for r in range(6):
            for level in range(3):
                for c in range(6):
                    cut[q * SLOT + r * 18 + level * 6 + c, (r * 3 + level) * 24 + 6 * q + c] = 1
    return cut


def unpack_matrix():
    pick = np.zeros((256, 256), np.float32)
    for s in range(16):
        for r in range(12):
            pick[12 * s + r, 16 * s + r] = 1
        for r in range(4):
            pick[192 + 4 * s + r, 16 * s + 12 + r] = 1
    return pick


class Place:
    def __init__(self):
        self.lon = lax.axis_index("lon")
        self.lat = lax.axis_index("lat")
        self.zlo = self.lon // 8
        self.x = (self.lon // 2) % 4
        self.core = self.lon % 2
        self.y = self.lat // 2
        self.zhi = self.lat % 2
        self.z = self.zhi * 2 + self.zlo

    def at(self, x=None, y=None, z=None, core=None):
        x = self.x if x is None else x
        y = self.y if y is None else y
        z = self.z if z is None else z
        core = self.core if core is None else core
        return (((z % 2) * 4 + x) * 2 + core, y * 2 + z // 2)

    def along(self, dim, step):
        there = (getattr(self, dim) + step) % 4
        return there, self.at(**{dim: there})

    def beside(self, east, south):
        return ((self.lon + east + 16) % 16, (self.lat + south + 8) % 8)


def token_regions(reg_row, half):
    def row_of(tok):
        quarter = tok // SLOT
        inside = tok - quarter * SLOT
        row = (quarter // 2) * 6 + inside // 18
        return jnp.where(inside < 108, row + 12 * half, 127)

    cols = lax.broadcasted_iota(jnp.int32, (N, 128), 1)
    toks = lax.broadcasted_iota(jnp.int32, (N, 128), 0)
    hot = (row_of(toks) == cols).astype(F32)
    col = jnp.sum(hot * reg_row, axis=1, keepdims=True)
    row = nt(jnp.broadcast_to(reg_row, (8, 128)).astype(BF), hot.astype(BF))[0:1]
    return col, row


def normalised(x):
    xf = x.astype(F32)
    centre = xf - jnp.mean(xf, axis=-1, keepdims=True)
    inverse = lax.rsqrt(jnp.mean(centre * centre, axis=-1, keepdims=True) + EPSILON)
    return centre * inverse, inverse


def mask_of(reg_row, half, bias):
    col, row = token_regions(reg_row, half)
    bias[...] = jnp.where(col == row, 0.0, -1e30)


def window(w, xg, wq, wp, normed_s, att_s, gqkv_s, qkv_s, ga_s, bias, r_s, t_s):
    normed = normed_s[w]
    qkv_s[:, :512] = nt(normed, wq[0:512, :]).astype(BF) * jnp.asarray(0.125, BF)
    qkv_s[:, 512:1024] = nt(normed, wq[512:1024, :]).astype(BF)
    qkv_s[:, 1024:] = nt(normed, wq[1024:, :]).astype(BF)
    ga_s[...] = nn(xg[1, w].reshape(N, C), wp[...]).astype(BF)
    low = lax.broadcasted_iota(jnp.int32, (N, 128), 1) < 64

    def pair(ref, base, head):
        o = base + 128 * (head // 2)
        return ref[:, o : o + 128]

    def alone(v, head):
        return jnp.where(low if head % 2 == 0 else jnp.logical_not(low), v, jnp.zeros_like(v))

    def weigh(head, b):
        query = alone(pair(qkv_s, 0, head), head)[b : b + BLK]
        grad = alone(pair(ga_s, 0, head), head)[b : b + BLK]
        s = nt(query, pair(qkv_s, 512, head))
        dp = nt(grad, pair(qkv_s, 1024, head))
        s = s + bias[b : b + BLK, :]
        m = jnp.max(s, axis=-1, keepdims=True)
        e = jnp.exp(s - m)
        p = e * (1.0 / jnp.sum(e, axis=-1, keepdims=True))
        r_s[head % 2, b : b + BLK, :] = p.astype(BF)
        inner = jnp.sum(dp * p, axis=-1, keepdims=True)
        t_s[head % 2, b : b + BLK, :] = (p * (dp - inner)).astype(BF)

    sums = {}

    def mix(head, part):
        r, t = r_s.at[head % 2], t_s.at[head % 2]
        if part == 0:
            sums[head, 0] = nn(r[...], pair(qkv_s, 1024, head))
            sums[head, 1] = nn(t[...], pair(qkv_s, 512, head))
        else:
            sums[head, 2] = tn(t[...], pair(qkv_s, 0, head))
            sums[head, 3] = tn(r[...], pair(ga_s, 0, head))
        if head % 2 == 1:
            o = 128 * (head // 2)
            for i in (2 * part, 2 * part + 1):
                v = jnp.where(low, sums.pop((head - 1, i)), sums.pop((head, i)))
                if i == 0:
                    att_s[w, :, o : o + 128] = v.astype(BF)
                else:
                    v = v * 0.125 if i == 1 else v
                    at = 512 * (i - 1) + o
                    gqkv_s[w, :, at : at + 128] = v.astype(BF)

    for head in range(9):
        for n in range(2):
            if head < 8:
                weigh(head, n * BLK)
            if head > 0:
                mix(head - 1, n)


def finish(w, xg, wq, wp, ow, att_s, gqkv_s):
    ow[0, w] = nt(att_s[w], wp[...]).astype(BF).reshape(4, SLOT, C)
    grad = nn(gqkv_s[w], wq[...])
    normal, inverse = normalised(xg[0, w].reshape(N, C))
    grad = inverse * (
        grad
        - jnp.mean(grad, axis=-1, keepdims=True)
        - normal * jnp.mean(grad * normal, axis=-1, keepdims=True)
    )
    ow[1, w] = grad.astype(BF).reshape(4, SLOT, C)


def kernel(
    f_hbm, g_hbm, reg_hbm, wq_hbm, wp_hbm, cut_hbm, paste_hbm, pick_hbm, pack_hbm,
    fo_ref, go_ref, qo_ref, po_ref,
    f_ref, g_ref, cut_ref, paste_ref, pick_ref, pack_ref, wq_ref, wp_ref, reg_ref, load_sem, store_sem,
    own_s, wg, wq, wp, stage, xg, reg_s, ow, rq,
    normed_s, att_s, gqkv_s, qkv_s, ga_s, bias_s, r_s, t_s,
    gw_s, pk, rc, h0, rb0, h1, rb1, h2, rb2,
    ag_a, ag_b, in_a, in_b, out_a, out_b, rc_a, rc_b, rs_a, rs_b,
):
    me = Place()
    sibling = me.at(core=1 - me.core)

    def copy(src, dst, a, b, device):
        return pltpu.make_async_remote_copy(
            src_ref=src, dst_ref=dst, send_sem=a, recv_sem=b, device_id=device, device_id_type=MESH
        )

    barrier = pltpu.get_barrier_semaphore()
    greeted = [me.along(d, s)[1] for d in ("x", "y", "z") for s in (1, 2, 3)] + [sibling]
    greeted += [me.beside(*o) for o in ((-1, 0), (1, 0), (0, -1), (0, 1), (1, 1), (-1, -1))]
    for device in greeted:
        pl.semaphore_signal(barrier, inc=1, device_id=device, device_id_type=MESH)

    loads = [
        pltpu.make_async_copy(src, dst, load_sem.at[n])
        for n, (src, dst) in enumerate(
            (
                (f_hbm, f_ref), (g_hbm, g_ref), (cut_hbm, cut_ref),
                (pick_hbm, pick_ref), (paste_hbm, paste_ref), (pack_hbm, pack_ref),
                (wq_hbm, wq_ref), (wp_hbm, wp_ref), (reg_hbm, reg_ref),
            )
        )
    ]
    for c in loads[6:] + loads[:6]:
        c.start()

    loads[6].wait()
    loads[7].wait()
    own_s[0:12, :] = wq_ref[...].astype(F32)
    own_s[12:16, :] = wp_ref[...].astype(F32)
    for k in range(4):
        outer, inner = (getattr(me, d) for d in AG_ORDER[k][:0:-1])
        wg[k, me.core, outer, inner, me.z] = own_s[:, 128 * k : 128 * k + 128].astype(BF)
    loads[8].wait()
    lane = lax.broadcasted_iota(jnp.int32, (8, 128), 1)
    regions = jnp.zeros((8, 128), jnp.int32)
    for n in range(24):
        regions = jnp.where(lane == n, reg_ref[n] + 1, regions)
    reg_s[0] = regions.astype(F32)
    pl.semaphore_wait(barrier, len(greeted))

    every = slice(None)

    def held(k, done, **fixed):
        own = (every if d in done else fixed.get(d, getattr(me, d)) for d in AG_ORDER[k][::-1])
        return wg.at[(k, me.core, *own)]

    gathers = []
    forwards = []

    def forward(k, number, part):
        c = copy(part, part, ag_a.at[36 + 4 * k + number], ag_b.at[36 + 4 * k + number], sibling)
        c.start()
        forwards.append(c)

    def gather_step(stage_index):
        for k in range(4):
            if stage_index > 0:
                for c in gathers[-4]:
                    c.wait_recv()
            order = AG_ORDER[k]
            part = held(k, order[:stage_index])
            started = []
            for step in (1, 3, 2):
                sem = k * 9 + stage_index * 3 + step - 1
                c = copy(part, part, ag_a.at[sem], ag_b.at[sem], me.along(order[stage_index], step)[1])
                c.start()
                started.append(c)
            gathers.append(started)
            if stage_index == 2:
                forward(k, 0, part)

    def gather_end():
        for half in range(2):
            for n, step in enumerate((1, 3, 2)):
                for k in (2 * half, 2 * half + 1):
                    gathers[k - 4][n].wait_recv()
                    dim = AG_ORDER[k][2]
                    forward(k, step, held(k, AG_ORDER[k][:2], **{dim: me.along(dim, 4 - step)[0]}))

    halos = {}

    def cut(qi, moves):
        for a, ref in ((0, f_ref), (1, g_ref)):
            rows = nn(cut_ref[...], ref[432 * qi : 432 * qi + 432, :]).astype(BF)
            for qj in range(4):
                quarter = rows[SLOT * qj : SLOT * qj + SLOT]
                where = moves[qj]
                if where[0] == "own":
                    xg[a, where[1], where[2]] = quarter
                else:
                    stage[a, where[1]] = quarter

    def send_in(name, slots, w, first, count, device, sem):
        c = copy(
            stage.at[:, pl.ds(slots, count)], xg.at[:, w, pl.ds(first, count)], in_a.at[sem], in_b.at[sem], device
        )
        c.start()
        halos.setdefault(name, []).append(c)

    gather_step(0)
    for c in loads[:3]:
        c.wait()
    cut(1, (("out", 5), ("own", 0, 0), ("own", 0, 1), ("own", 1, 0)))
    gather_step(1)
    cut(2, (("out", 6), ("own", 0, 2), ("own", 0, 3), ("own", 1, 2)))
    normed_s[0] = normalised(xg[0, 0].reshape(N, C))[0].astype(BF)
    gather_step(2)
    mask_of(reg_s[0, 0:1, :], 0, bias_s.at[0])
    mask_of(reg_s[0, 0:1, :], 1, bias_s.at[1])
    cut(0, (("own", 3, 3), ("out", 0), ("out", 1), ("out", 2)))
    send_in("s", 0, 2, 2, 2, me.beside(0, -1), 0)
    cut(3, (("out", 3), ("own", 2, 0), ("own", 2, 1), ("out", 4)))
    gather_end()
    send_in("e", 5, 1, 1, 1, me.beside(-1, 0), 4)
    send_in("e", 6, 1, 3, 1, me.beside(-1, 0), 5)
    send_in("c", 2, 3, 2, 1, me.beside(1, 0), 1)
    c = copy(reg_s.at[0], reg_s.at[1], in_a.at[6], in_b.at[6], me.beside(0, 1))
    c.start()
    halos["c"].append(c)
    send_in("c", 3, 3, 1, 1, me.beside(0, 1), 2)
    send_in("c", 4, 3, 0, 1, me.beside(1, 1), 3)
    for c in loads[3:6]:
        c.wait()

    inside = [(core, y, zhi) for core in range(2) for y in range(4) for zhi in range(2)]

    def spot(k, j, core, y, zhi):
        z = 2 * zhi + j // 4
        return (k, core, y, j % 4, z) if AG_ORDER[k][2] == "y" else (k, core, j % 4, y, z)

    for half in range(2):
        mine_now = (forwards[2 * half : 2 * half + 2], forwards[4 + 6 * half : 10 + 6 * half])
        for c in mine_now[0] + mine_now[1]:
            c.wait_recv()

        def unpack(j, _):
            parts = [
                jnp.concatenate([wg[spot(k, j, *i)] for i in inside], axis=0) for k in (2 * half, 2 * half + 1)
            ]
            got = nn(pick_ref[...], jnp.concatenate(parts, axis=1)).astype(BF)
            wq[pl.ds(pl.multiple_of(192 * j, 64), 192), 256 * half : 256 * half + 256] = got[:192]
            wp[pl.ds(pl.multiple_of(64 * j, 64), 64), 256 * half : 256 * half + 256] = got[192:]
            return 0

        lax.fori_loop(0, 8, unpack, 0)

    def send_out(w, first, qi, qj, count, device, sem):
        return copy(
            ow.at[:, w, pl.ds(first, count)], rq.at[:, qi, pl.ds(qj, count)], out_a.at[sem], out_b.at[sem], device
        )

    returns = [
        send_out(2, 2, 0, 1, 2, me.beside(0, 1), 0),
        send_out(3, 2, 0, 3, 1, me.beside(-1, 0), 1),
        send_out(3, 1, 3, 0, 1, me.beside(0, -1), 2),
        send_out(3, 0, 3, 3, 1, me.beside(-1, -1), 3),
        send_out(1, 1, 1, 0, 1, me.beside(1, 0), 4),
        send_out(1, 3, 2, 0, 1, me.beside(1, 0), 5),
    ]
    leaves = {1: (4, 5), 2: (0,), 3: (3, 2, 1)}

    def turn(i, _):
        for step, name in ((1, "e"), (2, "s"), (3, "c")):

            @pl.when(i == step)
            def _():
                for c in halos[name]:
                    c.wait_recv()

        @pl.when(i > 0)
        def _():
            normed_s[i] = normalised(xg[0, i].reshape(N, C))[0].astype(BF)

        @pl.when(i == 3)
        def _():
            mask_of(reg_s[1, 0:1, :], 1, bias_s.at[2])

        bias = bias_s.at[jnp.maximum(i - 1, 0)]
        window(i, xg, wq, wp, normed_s, att_s, gqkv_s, qkv_s, ga_s, bias, r_s, t_s)

        @pl.when(i > 0)
        def _():
            finish(i, xg, wq, wp, ow, att_s, gqkv_s)

        for step in (1, 2, 3):

            @pl.when(i == step)
            def _():
                for number in leaves[step]:
                    returns[number].start()

        return 0

    lax.fori_loop(0, 4, turn, 0)

    crossing = [copy(pk.at[k, 1 - me.core], rc.at[k], rc_a.at[k], rc_b.at[k], sibling) for k in range(4)]
    reduces = []

    def reduce_step(stage_index, k):
        order = RS_ORDER[k]
        started = []
        for step in (2, 1, 3):
            there, device = me.along(order[stage_index], step)
            src = (h0, h1, h2)[stage_index].at[k, there]
            dst = (rb0, rb1, rb2)[stage_index].at[k, step - 1]
            sem = k * 9 + stage_index * 3 + step - 1
            c = copy(src, dst, rs_a.at[sem], rs_b.at[sem], device)
            c.start()
            started.append(c)
        reduces.append(started)

    def reduce_take(stage_index, k):
        for c in reduces[4 * stage_index + k]:
            c.wait_recv()
        got = (rb0, rb1, rb2)[stage_index]
        total = (h0, h1, h2)[stage_index][k, getattr(me, RS_ORDER[k][stage_index])].astype(F32)
        for step in range(3):
            total = total + got[k, step].astype(F32)
        if stage_index < 2:
            (h1, h2)[stage_index][k] = total.astype(BF)
        else:
            own_s[:, 128 * k : 128 * k + 128] = total

    def merge(k):
        crossing[k].wait_recv()
        h0[k] = (pk[k, me.core].astype(F32) + rc[k].astype(F32)).astype(BF)
        reduce_step(0, k)

    for half in range(2):
        cols = slice(256 * half, 256 * half + 256)
        normed = normed_s[:, :, cols].reshape(4 * N, 256)

        def weight_chunk(i, _):
            o = pl.multiple_of(i * 256, 256)
            left = gqkv_s[:, :, pl.ds(o, 256)].reshape(4 * N, 256)
            gw_s[pl.ds(o, 256), cols] = (tn(left, normed) * FACTOR).astype(BF)
            return 0

        lax.fori_loop(0, 6, weight_chunk, 0)
        right = att_s[:, :, cols].reshape(4 * N, 256)
        gw_s[1536:2048, cols] = (tn(xg[1].reshape(4 * N, C), right) * FACTOR).astype(BF)
        if half == 1:
            merge(0)
            merge(1)

        def pack(j, _):
            rows = jnp.concatenate(
                [
                    gw_s[pl.ds(pl.multiple_of(192 * j, 64), 192), 256 * half : 256 * half + 256],
                    gw_s[pl.ds(pl.multiple_of(1536 + 64 * j, 64), 64), 256 * half : 256 * half + 256],
                ],
                axis=0,
            )
            got = nn(pack_ref[...], rows).astype(BF)
            for n, i in enumerate(inside):
                for k in range(2):
                    pk[spot(2 * half + k, j, *i)] = got[16 * n : 16 * n + 16, 128 * k : 128 * k + 128]
            return 0

        lax.fori_loop(0, 8, pack, 0)
        crossing[2 * half].start()
        crossing[2 * half + 1].start()

    mine = {
        (1, 1): (0, 0), (1, 2): (0, 1), (2, 1): (0, 2), (2, 2): (0, 3), (1, 3): (1, 0),
        (2, 3): (1, 2), (3, 1): (2, 0), (3, 2): (2, 1), (0, 0): (3, 3),
    }

    stores = []

    def paste(qi):
        for a, ref, out in ((0, f_ref, fo_ref), (1, g_ref, go_ref)):
            quarters = []
            for qj in range(4):
                if (qi, qj) in mine:
                    quarters.append(ow[(a,) + mine[(qi, qj)]])
                else:
                    quarters.append(rq[a, qi, qj])
            back = nn(paste_ref[...], jnp.concatenate(quarters, axis=0))
            rows = slice(432 * qi, 432 * qi + 432)
            ref[rows, :] = (ref[rows, :].astype(F32) + back).astype(BF)
            c = pltpu.make_async_copy(ref.at[rows], out.at[rows], store_sem.at[2 * qi + a])
            c.start()
            stores.append(c)

    merge(2)
    merge(3)
    finish(0, xg, wq, wp, ow, att_s, gqkv_s)
    for n in (4, 5):
        returns[n].wait_recv()
    paste(1)
    paste(2)
    for k in range(4):
        reduce_take(0, k)
        reduce_step(1, k)
    for n in range(4):
        returns[n].wait_recv()
    paste(0)
    for k in range(4):
        reduce_take(1, k)
        reduce_step(2, k)
    paste(3)
    for k in range(4):
        reduce_take(2, k)
    for c in stores:
        c.wait()
    qo_ref[...] = own_s[0:12, :]
    po_ref[...] = own_s[12:16, :]

    for started in gathers + reduces + [returns, forwards, crossing] + list(halos.values()):
        for c in started:
            c.wait_send()


def settle(fo, go, qo, po, f_out, g_out, q_out, p_out, f_s, g_s, q_s, p_s, in_sem, out_sem):
    parts = [(qo, q_s, q_out), (po, p_s, p_out)]
    for n in range(0, 1728, 432):
        rows = pl.ds(n, 432)
        parts.append((fo.at[rows], f_s.at[rows], f_out.at[rows]))
        parts.append((go.at[rows], g_s.at[rows], g_out.at[rows]))
    inward = [pltpu.make_async_copy(a, b, in_sem.at[n]) for n, (a, b, c) in enumerate(parts)]
    outward = [pltpu.make_async_copy(b, c, out_sem.at[n]) for n, (a, b, c) in enumerate(parts)]
    for c in inward:
        c.start()
    for c, d in zip(inward, outward):
        c.wait()
        d.start()
    for d in outward:
        d.wait()


def shards(fields, region_ids, w_qkv, w_proj, grad_output):
    tokens = 24 * 24 * 3
    flat = fields.transpose(0, 2, 1, 3).reshape(tokens, C)
    grad = grad_output.transpose(0, 2, 1, 3).reshape(tokens, C)
    cut = cut_matrix()
    pick = unpack_matrix()
    vm = pl.BlockSpec(memory_space=pltpu.VMEM)
    hbm = pl.BlockSpec(memory_space=pltpu.HBM)
    anywhere = pl.BlockSpec(memory_space=pl.ANY)
    shape = jax.ShapeDtypeStruct
    dma = pltpu.SemaphoreType.DMA
    fo, go, qo, po = pl.pallas_call(
        kernel,
        out_shape=(shape((tokens, C), BF), shape((tokens, C), BF), shape((12, C), F32), shape((4, C), F32)),
        in_specs=[hbm] * 9,
        out_specs=[anywhere] * 2 + [vm] * 2,
        scratch_shapes=[
            pltpu.VMEM((tokens, C), BF),
            pltpu.VMEM((tokens, C), BF),
            pltpu.VMEM((N, 432), BF),
            pltpu.VMEM((432, N), BF),
            pltpu.VMEM((256, 256), BF),
            pltpu.VMEM((256, 256), BF),
            pltpu.VMEM((12, C), BF),
            pltpu.VMEM((4, C), BF),
            pltpu.SMEM((24,), jnp.int32),
            dma((9,)),
            dma((8,)),
            pltpu.VMEM((16, C), F32),
            pltpu.VMEM((4, 2, 4, 4, 4, 16, 128), BF),
            pltpu.VMEM((1536, C), BF),
            pltpu.VMEM((C, C), BF),
            pltpu.VMEM((2, 7, SLOT, C), BF),
            pltpu.VMEM((2, 4, 4, SLOT, C), BF),
            pltpu.VMEM((2, 8, 128), F32),
            pltpu.VMEM((2, 4, 4, SLOT, C), BF),
            pltpu.VMEM((2, 4, 4, SLOT, C), BF),
            pltpu.VMEM((4, N, C), BF),
            pltpu.VMEM((4, N, C), BF),
            pltpu.VMEM((4, N, 3 * C), BF),
            pltpu.VMEM((N, 3 * C), BF),
            pltpu.VMEM((N, C), BF),
            pltpu.VMEM((3, N, N), F32),
            pltpu.VMEM((2, N, N), BF),
            pltpu.VMEM((2, N, N), BF),
            pltpu.VMEM((2048, C), BF),
            pltpu.VMEM((4, 2, 4, 4, 4, 16, 128), BF),
            pltpu.VMEM((4, 4, 4, 4, 16, 128), BF),
            pltpu.VMEM((4, 4, 4, 4, 16, 128), BF),
            pltpu.VMEM((4, 3, 4, 4, 16, 128), BF),
            pltpu.VMEM((4, 4, 4, 16, 128), BF),
            pltpu.VMEM((4, 3, 4, 16, 128), BF),
            pltpu.VMEM((4, 4, 16, 128), BF),
            pltpu.VMEM((4, 3, 16, 128), BF),
            dma((52,)), dma((52,)), dma((7,)), dma((7,)), dma((6,)), dma((6,)),
            dma((4,)), dma((4,)), dma((36,)), dma((36,)),
        ],
        compiler_params=pltpu.CompilerParams(
            collective_id=0, has_side_effects=True, vmem_limit_bytes=56 * 1024 * 1024
        ),
        name="block",
    )(
        flat, grad, region_ids, w_qkv, w_proj,
        jnp.asarray(cut, BF), jnp.asarray(cut.T, BF), jnp.asarray(pick, BF), jnp.asarray(pick.T, BF),
    )
    block_out, grad_fields, qo, po = pl.pallas_call(
        settle,
        out_shape=(shape((tokens, C), BF), shape((tokens, C), BF), shape((12, C), F32), shape((4, C), F32)),
        in_specs=[anywhere] * 4,
        out_specs=[anywhere] * 4,
        scratch_shapes=[
            pltpu.VMEM((tokens, C), BF),
            pltpu.VMEM((tokens, C), BF),
            pltpu.VMEM((12, C), F32),
            pltpu.VMEM((4, C), F32),
            dma((10,)),
            dma((10,)),
        ],
        compiler_params=pltpu.CompilerParams(vmem_limit_bytes=56 * 1024 * 1024),
        name="settle",
    )(fo, go, qo, po)
    block_out = block_out.reshape(24, 3, 24, C).transpose(0, 2, 1, 3)
    grad_fields = grad_fields.reshape(24, 3, 24, C).transpose(0, 2, 1, 3)
    return block_out, grad_fields, qo, po


def solution(mesh):
    return jax.shard_map(
        shards,
        mesh=mesh,
        in_specs=(
            P("lat", "lon", None, None), P("lat"), P(("lon", "lat"), None), P(("lon", "lat"), None),
            P("lat", "lon", None, None),
        ),
        out_specs=(
            P("lat", "lon", None, None), P("lat", "lon", None, None),
            P(("lon", "lat"), None), P(("lon", "lat"), None),
        ),
        check_vma=False,
    )
```

```python
import jax
import jax.numpy as jnp
import numpy as np
from jax import lax
from jax.experimental import pallas as pl
from jax.experimental.pallas import tpu as pltpu
from jax.sharding import PartitionSpec as P

F32 = jnp.float32
BF = jnp.bfloat16
EPSILON = 1e-05
SLOT = 112
N = 4 * SLOT
C = 512
BLK = 224
FACTOR = float(221184) ** (-0.5)
MESH = pl.DeviceIdType.MESH
AG_ORDER = (("z", "x", "y"), ("z", "y", "x"), ("z", "x", "y"), ("z", "y", "x"))
RS_ORDER = (("y", "x", "z"), ("x", "y", "z"), ("y", "x", "z"), ("x", "y", "z"))


def nt(a, b):
    return lax.dot_general(a, b, (((1,), (1,)), ((), ())), preferred_element_type=F32)


def nn(a, b):
    return lax.dot_general(a, b, (((1,), (0,)), ((), ())), preferred_element_type=F32)


def tn(a, b):
    return lax.dot_general(a, b, (((0,), (0,)), ((), ())), preferred_element_type=F32)


def cut_matrix():
    cut = np.zeros((N, 432), np.float32)
    for q in range(4):
        for r in range(6):
            for level in range(3):
                for c in range(6):
                    cut[q * SLOT + r * 18 + level * 6 + c, (r * 3 + level) * 24 + 6 * q + c] = 1
    return cut


def unpack_matrix():
    pick = np.zeros((256, 256), np.float32)
    for s in range(16):
        for r in range(12):
            pick[12 * s + r, 16 * s + r] = 1
        for r in range(4):
            pick[192 + 4 * s + r, 16 * s + 12 + r] = 1
    return pick


class Place:
    def __init__(self):
        self.lon = lax.axis_index("lon")
        self.lat = lax.axis_index("lat")
        self.zlo = self.lon // 8
        self.x = (self.lon // 2) % 4
        self.core = self.lon % 2
        self.y = self.lat // 2
        self.zhi = self.lat % 2
        self.z = self.zhi * 2 + self.zlo

    def at(self, x=None, y=None, z=None, core=None):
        x = self.x if x is None else x
        y = self.y if y is None else y
        z = self.z if z is None else z
        core = self.core if core is None else core
        return (((z % 2) * 4 + x) * 2 + core, y * 2 + z // 2)

    def along(self, dim, step):
        there = (getattr(self, dim) + step) % 4
        return there, self.at(**{dim: there})

    def beside(self, east, south):
        return ((self.lon + east + 16) % 16, (self.lat + south + 8) % 8)


def token_regions(reg_row, half):
    def row_of(tok):
        quarter = tok // SLOT
        inside = tok - quarter * SLOT
        row = (quarter // 2) * 6 + inside // 18
        return jnp.where(inside < 108, row + 12 * half, 127)

    cols = lax.broadcasted_iota(jnp.int32, (N, 128), 1)
    toks = lax.broadcasted_iota(jnp.int32, (N, 128), 0)
    hot = (row_of(toks) == cols).astype(F32)
    col = jnp.sum(hot * reg_row, axis=1, keepdims=True)
    row = nt(jnp.broadcast_to(reg_row, (8, 128)).astype(BF), hot.astype(BF))[0:1]
    return col, row


def normalised(x):
    xf = x.astype(F32)
    centre = xf - jnp.mean(xf, axis=-1, keepdims=True)
    inverse = lax.rsqrt(jnp.mean(centre * centre, axis=-1, keepdims=True) + EPSILON)
    return centre * inverse, inverse


def mask_of(reg_row, half, bias):
    col, row = token_regions(reg_row, half)
    bias[...] = jnp.where(col == row, 0.0, -1e30)


def window(w, xg, wq, wp, normed_s, att_s, gqkv_s, qkv_s, ga_s, bias, r_s, t_s):
    normed = normed_s[w]
    qkv_s[:, :512] = nt(normed, wq[0:512, :]).astype(BF) * jnp.asarray(0.125, BF)
    qkv_s[:, 512:1024] = nt(normed, wq[512:1024, :]).astype(BF)
    qkv_s[:, 1024:] = nt(normed, wq[1024:, :]).astype(BF)
    ga_s[...] = nn(xg[1, w].reshape(N, C), wp[...]).astype(BF)
    low = lax.broadcasted_iota(jnp.int32, (N, 128), 1) < 64

    def pair(ref, base, head):
        o = base + 128 * (head // 2)
        return ref[:, o : o + 128]

    def alone(v, head):
        return jnp.where(low if head % 2 == 0 else jnp.logical_not(low), v, jnp.zeros_like(v))

    def weigh(head, b):
        query = alone(pair(qkv_s, 0, head), head)[b : b + BLK]
        grad = alone(pair(ga_s, 0, head), head)[b : b + BLK]
        s = nt(query, pair(qkv_s, 512, head))
        dp = nt(grad, pair(qkv_s, 1024, head))
        s = s + bias[b : b + BLK, :]
        m = jnp.max(s, axis=-1, keepdims=True)
        e = jnp.exp(s - m)
        p = e * (1.0 / jnp.sum(e, axis=-1, keepdims=True))
        r_s[head % 2, b : b + BLK, :] = p.astype(BF)
        inner = jnp.sum(dp * p, axis=-1, keepdims=True)
        t_s[head % 2, b : b + BLK, :] = (p * (dp - inner)).astype(BF)

    sums = {}

    def mix(head, part):
        r, t = r_s.at[head % 2], t_s.at[head % 2]
        if part == 0:
            sums[head, 0] = nn(r[...], pair(qkv_s, 1024, head))
            sums[head, 1] = nn(t[...], pair(qkv_s, 512, head))
        else:
            sums[head, 2] = tn(t[...], pair(qkv_s, 0, head))
            sums[head, 3] = tn(r[...], pair(ga_s, 0, head))
        if head % 2 == 1:
            o = 128 * (head // 2)
            for i in (2 * part, 2 * part + 1):
                v = jnp.where(low, sums.pop((head - 1, i)), sums.pop((head, i)))
                if i == 0:
                    att_s[w, :, o : o + 128] = v.astype(BF)
                else:
                    v = v * 0.125 if i == 1 else v
                    at = 512 * (i - 1) + o
                    gqkv_s[w, :, at : at + 128] = v.astype(BF)

    for head in range(9):
        for n in range(2):
            if head < 8:
                weigh(head, n * BLK)
            if head > 0:
                mix(head - 1, n)


def finish(w, xg, wq, wp, ow, att_s, gqkv_s):
    ow[0, w] = nt(att_s[w], wp[...]).astype(BF).reshape(4, SLOT, C)
    grad = nn(gqkv_s[w], wq[...])
    normal, inverse = normalised(xg[0, w].reshape(N, C))
    grad = inverse * (
        grad
        - jnp.mean(grad, axis=-1, keepdims=True)
        - normal * jnp.mean(grad * normal, axis=-1, keepdims=True)
    )
    ow[1, w] = grad.astype(BF).reshape(4, SLOT, C)


def kernel(
    f_hbm, g_hbm, reg_hbm, wq_hbm, wp_hbm, cut_hbm, paste_hbm, pick_hbm, pack_hbm,
    fo_ref, go_ref, qo_ref, po_ref,
    f_ref, g_ref, cut_ref, paste_ref, pick_ref, pack_ref, wq_ref, wp_ref, reg_ref, load_sem, store_sem,
    own_s, wg, wq, wp, stage, xg, reg_s, ow, rq,
    normed_s, att_s, gqkv_s, qkv_s, ga_s, bias_s, r_s, t_s,
    gw_s, pk, rc, h0, rb0, h1, rb1, h2, rb2,
    ag_a, ag_b, in_a, in_b, out_a, out_b, rc_a, rc_b, rs_a, rs_b,
):
    me = Place()
    sibling = me.at(core=1 - me.core)

    def copy(src, dst, a, b, device):
        return pltpu.make_async_remote_copy(
            src_ref=src, dst_ref=dst, send_sem=a, recv_sem=b, device_id=device, device_id_type=MESH
        )

    barrier = pltpu.get_barrier_semaphore()
    greeted = [me.along(d, s)[1] for d in ("x", "y", "z") for s in (1, 2, 3)] + [sibling]
    greeted += [me.beside(*o) for o in ((-1, 0), (1, 0), (0, -1), (0, 1), (1, 1), (-1, -1))]
    for device in greeted:
        pl.semaphore_signal(barrier, inc=1, device_id=device, device_id_type=MESH)

    loads = [
        pltpu.make_async_copy(src, dst, load_sem.at[n])
        for n, (src, dst) in enumerate(
            (
                (f_hbm, f_ref), (g_hbm, g_ref), (cut_hbm, cut_ref),
                (pick_hbm, pick_ref), (paste_hbm, paste_ref), (pack_hbm, pack_ref),
                (wq_hbm, wq_ref), (wp_hbm, wp_ref), (reg_hbm, reg_ref),
            )
        )
    ]
    for c in loads[6:] + loads[:6]:
        c.start()

    loads[6].wait()
    loads[7].wait()
    own_s[0:12, :] = wq_ref[...].astype(F32)
    own_s[12:16, :] = wp_ref[...].astype(F32)
    for k in range(4):
        outer, inner = (getattr(me, d) for d in AG_ORDER[k][:0:-1])
        wg[k, me.core, outer, inner, me.z] = own_s[:, 128 * k : 128 * k + 128].astype(BF)
    pl.semaphore_wait(barrier, len(greeted))

    every = slice(None)

    def held(k, done, **fixed):
        own = (every if d in done else fixed.get(d, getattr(me, d)) for d in AG_ORDER[k][::-1])
        return wg.at[(k, me.core, *own)]

    gathers = []
    forwards = []

    def forward(k, number, part):
        c = copy(part, part, ag_a.at[36 + 4 * k + number], ag_b.at[36 + 4 * k + number], sibling)
        c.start()
        forwards.append(c)

    def gather_step(stage_index):
        for k in range(4):
            if stage_index > 0:
                for c in gathers[-4]:
                    c.wait_recv()
            order = AG_ORDER[k]
            part = held(k, order[:stage_index])
            started = []
            for step in (1, 3, 2):
                sem = k * 9 + stage_index * 3 + step - 1
                c = copy(part, part, ag_a.at[sem], ag_b.at[sem], me.along(order[stage_index], step)[1])
                c.start()
                started.append(c)
            gathers.append(started)
            if stage_index == 2:
                forward(k, 0, part)

    def gather_end():
        for half in range(2):
            for n, step in enumerate((1, 3, 2)):
                for k in (2 * half, 2 * half + 1):
                    gathers[k - 4][n].wait_recv()
                    dim = AG_ORDER[k][2]
                    forward(k, step, held(k, AG_ORDER[k][:2], **{dim: me.along(dim, 4 - step)[0]}))

    halos = {}

    def cut(qi, moves):
        for a, ref in ((0, f_ref), (1, g_ref)):
            rows = nn(cut_ref[...], ref[432 * qi : 432 * qi + 432, :]).astype(BF)
            for qj in range(4):
                quarter = rows[SLOT * qj : SLOT * qj + SLOT]
                where = moves[qj]
                if where[0] == "own":
                    xg[a, where[1], where[2]] = quarter
                else:
                    stage[a, where[1]] = quarter

    def send_in(name, slots, w, first, count, device, sem):
        c = copy(
            stage.at[:, pl.ds(slots, count)], xg.at[:, w, pl.ds(first, count)], in_a.at[sem], in_b.at[sem], device
        )
        c.start()
        halos.setdefault(name, []).append(c)

    gather_step(0)
    loads[8].wait()
    lane = lax.broadcasted_iota(jnp.int32, (8, 128), 1)
    regions = jnp.zeros((8, 128), jnp.int32)
    for n in range(24):
        regions = jnp.where(lane == n, reg_ref[n] + 1, regions)
    reg_s[0] = regions.astype(F32)
    for c in loads[:3]:
        c.wait()
    cut(1, (("out", 5), ("own", 0, 0), ("own", 0, 1), ("own", 1, 0)))
    gather_step(1)
    cut(2, (("out", 6), ("own", 0, 2), ("own", 0, 3), ("own", 1, 2)))
    normed_s[0] = normalised(xg[0, 0].reshape(N, C))[0].astype(BF)
    gather_step(2)
    mask_of(reg_s[0, 0:1, :], 0, bias_s.at[0])
    mask_of(reg_s[0, 0:1, :], 1, bias_s.at[1])
    cut(0, (("own", 3, 3), ("out", 0), ("out", 1), ("out", 2)))
    send_in("s", 0, 2, 2, 2, me.beside(0, -1), 0)
    cut(3, (("out", 3), ("own", 2, 0), ("own", 2, 1), ("out", 4)))
    gather_end()
    send_in("e", 5, 1, 1, 1, me.beside(-1, 0), 4)
    send_in("e", 6, 1, 3, 1, me.beside(-1, 0), 5)
    send_in("c", 2, 3, 2, 1, me.beside(1, 0), 1)
    c = copy(reg_s.at[0], reg_s.at[1], in_a.at[6], in_b.at[6], me.beside(0, 1))
    c.start()
    halos["c"].append(c)
    send_in("c", 3, 3, 1, 1, me.beside(0, 1), 2)
    send_in("c", 4, 3, 0, 1, me.beside(1, 1), 3)
    for c in loads[3:6]:
        c.wait()

    inside = [(core, y, zhi) for core in range(2) for y in range(4) for zhi in range(2)]

    def spot(k, j, core, y, zhi):
        z = 2 * zhi + j // 4
        return (k, core, y, j % 4, z) if AG_ORDER[k][2] == "y" else (k, core, j % 4, y, z)

    for half in range(2):
        mine_now = (forwards[2 * half : 2 * half + 2], forwards[4 + 6 * half : 10 + 6 * half])
        for c in mine_now[0] + mine_now[1]:
            c.wait_recv()

        def unpack(j, _):
            parts = [
                jnp.concatenate([wg[spot(k, j, *i)] for i in inside], axis=0) for k in (2 * half, 2 * half + 1)
            ]
            got = nn(pick_ref[...], jnp.concatenate(parts, axis=1)).astype(BF)
            wq[pl.ds(pl.multiple_of(192 * j, 64), 192), 256 * half : 256 * half + 256] = got[:192]
            wp[pl.ds(pl.multiple_of(64 * j, 64), 64), 256 * half : 256 * half + 256] = got[192:]
            return 0

        lax.fori_loop(0, 8, unpack, 0)

    def send_out(w, first, qi, qj, count, device, sem):
        return copy(
            ow.at[:, w, pl.ds(first, count)], rq.at[:, qi, pl.ds(qj, count)], out_a.at[sem], out_b.at[sem], device
        )

    returns = [
        send_out(2, 2, 0, 1, 2, me.beside(0, 1), 0),
        send_out(3, 2, 0, 3, 1, me.beside(-1, 0), 1),
        send_out(3, 1, 3, 0, 1, me.beside(0, -1), 2),
        send_out(3, 0, 3, 3, 1, me.beside(-1, -1), 3),
        send_out(1, 1, 1, 0, 1, me.beside(1, 0), 4),
        send_out(1, 3, 2, 0, 1, me.beside(1, 0), 5),
    ]
    leaves = {1: (4, 5), 2: (0,), 3: (3, 2, 1)}

    def turn(i, _):
        for step, name in ((1, "e"), (2, "s"), (3, "c")):

            @pl.when(i == step)
            def _():
                for c in halos[name]:
                    c.wait_recv()

        @pl.when(i > 0)
        def _():
            normed_s[i] = normalised(xg[0, i].reshape(N, C))[0].astype(BF)

        @pl.when(i == 3)
        def _():
            mask_of(reg_s[1, 0:1, :], 1, bias_s.at[2])

        bias = bias_s.at[jnp.maximum(i - 1, 0)]
        window(i, xg, wq, wp, normed_s, att_s, gqkv_s, qkv_s, ga_s, bias, r_s, t_s)

        @pl.when(i > 0)
        def _():
            finish(i, xg, wq, wp, ow, att_s, gqkv_s)

        for step in (1, 2, 3):

            @pl.when(i == step)
            def _():
                for number in leaves[step]:
                    returns[number].start()

        return 0

    lax.fori_loop(0, 4, turn, 0)

    crossing = [copy(pk.at[k, 1 - me.core], rc.at[k], rc_a.at[k], rc_b.at[k], sibling) for k in range(4)]
    reduces = []

    def reduce_step(stage_index, k):
        order = RS_ORDER[k]
        started = []
        for step in (2, 1, 3):
            there, device = me.along(order[stage_index], step)
            src = (h0, h1, h2)[stage_index].at[k, there]
            dst = (rb0, rb1, rb2)[stage_index].at[k, step - 1]
            sem = k * 9 + stage_index * 3 + step - 1
            c = copy(src, dst, rs_a.at[sem], rs_b.at[sem], device)
            c.start()
            started.append(c)
        reduces.append(started)

    def reduce_take(stage_index, k):
        for c in reduces[4 * stage_index + k]:
            c.wait_recv()
        got = (rb0, rb1, rb2)[stage_index]
        total = (h0, h1, h2)[stage_index][k, getattr(me, RS_ORDER[k][stage_index])].astype(F32)
        for step in range(3):
            total = total + got[k, step].astype(F32)
        if stage_index < 2:
            (h1, h2)[stage_index][k] = total.astype(BF)
        else:
            own_s[:, 128 * k : 128 * k + 128] = total

    def merge(k):
        crossing[k].wait_recv()
        h0[k] = (pk[k, me.core].astype(F32) + rc[k].astype(F32)).astype(BF)
        reduce_step(0, k)

    for half in range(2):
        cols = slice(256 * half, 256 * half + 256)
        normed = normed_s[:, :, cols].reshape(4 * N, 256)

        def weight_chunk(i, _):
            o = pl.multiple_of(i * 256, 256)
            left = gqkv_s[:, :, pl.ds(o, 256)].reshape(4 * N, 256)
            gw_s[pl.ds(o, 256), cols] = (tn(left, normed) * FACTOR).astype(BF)
            return 0

        lax.fori_loop(0, 6, weight_chunk, 0)
        right = att_s[:, :, cols].reshape(4 * N, 256)
        gw_s[1536:2048, cols] = (tn(xg[1].reshape(4 * N, C), right) * FACTOR).astype(BF)
        if half == 1:
            merge(0)
            merge(1)

        def pack(j, _):
            rows = jnp.concatenate(
                [
                    gw_s[pl.ds(pl.multiple_of(192 * j, 64), 192), 256 * half : 256 * half + 256],
                    gw_s[pl.ds(pl.multiple_of(1536 + 64 * j, 64), 64), 256 * half : 256 * half + 256],
                ],
                axis=0,
            )
            got = nn(pack_ref[...], rows).astype(BF)
            for n, i in enumerate(inside):
                for k in range(2):
                    pk[spot(2 * half + k, j, *i)] = got[16 * n : 16 * n + 16, 128 * k : 128 * k + 128]
            return 0

        lax.fori_loop(0, 8, pack, 0)
        crossing[2 * half].start()
        crossing[2 * half + 1].start()

    mine = {
        (1, 1): (0, 0), (1, 2): (0, 1), (2, 1): (0, 2), (2, 2): (0, 3), (1, 3): (1, 0),
        (2, 3): (1, 2), (3, 1): (2, 0), (3, 2): (2, 1), (0, 0): (3, 3),
    }

    stores = []

    def paste(qi):
        for a, ref, out in ((0, f_ref, fo_ref), (1, g_ref, go_ref)):
            quarters = []
            for qj in range(4):
                if (qi, qj) in mine:
                    quarters.append(ow[(a,) + mine[(qi, qj)]])
                else:
                    quarters.append(rq[a, qi, qj])
            back = nn(paste_ref[...], jnp.concatenate(quarters, axis=0))
            rows = slice(432 * qi, 432 * qi + 432)
            ref[rows, :] = (ref[rows, :].astype(F32) + back).astype(BF)
            c = pltpu.make_async_copy(ref.at[rows], out.at[rows], store_sem.at[2 * qi + a])
            c.start()
            stores.append(c)

    merge(2)
    merge(3)
    finish(0, xg, wq, wp, ow, att_s, gqkv_s)
    for n in (4, 5):
        returns[n].wait_recv()
    paste(1)
    paste(2)
    for k in range(4):
        reduce_take(0, k)
        reduce_step(1, k)
    for n in range(4):
        returns[n].wait_recv()
    paste(0)
    for k in range(4):
        reduce_take(1, k)
        reduce_step(2, k)
    paste(3)
    for k in range(4):
        reduce_take(2, k)
    for c in stores:
        c.wait()
    qo_ref[...] = own_s[0:12, :]
    po_ref[...] = own_s[12:16, :]

    for started in gathers + reduces + [returns, forwards, crossing] + list(halos.values()):
        for c in started:
            c.wait_send()


def settle(fo, go, qo, po, f_out, g_out, q_out, p_out, f_s, g_s, q_s, p_s, in_sem, out_sem):
    parts = [(qo, q_s, q_out), (po, p_s, p_out)]
    for n in range(0, 1728, 432):
        rows = pl.ds(n, 432)
        parts.append((fo.at[rows], f_s.at[rows], f_out.at[rows]))
        parts.append((go.at[rows], g_s.at[rows], g_out.at[rows]))
    inward = [pltpu.make_async_copy(a, b, in_sem.at[n]) for n, (a, b, c) in enumerate(parts)]
    outward = [pltpu.make_async_copy(b, c, out_sem.at[n]) for n, (a, b, c) in enumerate(parts)]
    for c in inward:
        c.start()
    for c, d in zip(inward, outward):
        c.wait()
        d.start()
    for d in outward:
        d.wait()


def shards(fields, region_ids, w_qkv, w_proj, grad_output):
    tokens = 24 * 24 * 3
    flat = fields.transpose(0, 2, 1, 3).reshape(tokens, C)
    grad = grad_output.transpose(0, 2, 1, 3).reshape(tokens, C)
    cut = cut_matrix()
    pick = unpack_matrix()
    vm = pl.BlockSpec(memory_space=pltpu.VMEM)
    hbm = pl.BlockSpec(memory_space=pltpu.HBM)
    anywhere = pl.BlockSpec(memory_space=pl.ANY)
    shape = jax.ShapeDtypeStruct
    dma = pltpu.SemaphoreType.DMA
    fo, go, qo, po = pl.pallas_call(
        kernel,
        out_shape=(shape((tokens, C), BF), shape((tokens, C), BF), shape((12, C), F32), shape((4, C), F32)),
        in_specs=[hbm] * 9,
        out_specs=[anywhere] * 2 + [vm] * 2,
        scratch_shapes=[
            pltpu.VMEM((tokens, C), BF),
            pltpu.VMEM((tokens, C), BF),
            pltpu.VMEM((N, 432), BF),
            pltpu.VMEM((432, N), BF),
            pltpu.VMEM((256, 256), BF),
            pltpu.VMEM((256, 256), BF),
            pltpu.VMEM((12, C), BF),
            pltpu.VMEM((4, C), BF),
            pltpu.SMEM((24,), jnp.int32),
            dma((9,)),
            dma((8,)),
            pltpu.VMEM((16, C), F32),
            pltpu.VMEM((4, 2, 4, 4, 4, 16, 128), BF),
            pltpu.VMEM((1536, C), BF),
            pltpu.VMEM((C, C), BF),
            pltpu.VMEM((2, 7, SLOT, C), BF),
            pltpu.VMEM((2, 4, 4, SLOT, C), BF),
            pltpu.VMEM((2, 8, 128), F32),
            pltpu.VMEM((2, 4, 4, SLOT, C), BF),
            pltpu.VMEM((2, 4, 4, SLOT, C), BF),
            pltpu.VMEM((4, N, C), BF),
            pltpu.VMEM((4, N, C), BF),
            pltpu.VMEM((4, N, 3 * C), BF),
            pltpu.VMEM((N, 3 * C), BF),
            pltpu.VMEM((N, C), BF),
            pltpu.VMEM((3, N, N), F32),
            pltpu.VMEM((2, N, N), BF),
            pltpu.VMEM((2, N, N), BF),
            pltpu.VMEM((2048, C), BF),
            pltpu.VMEM((4, 2, 4, 4, 4, 16, 128), BF),
            pltpu.VMEM((4, 4, 4, 4, 16, 128), BF),
            pltpu.VMEM((4, 4, 4, 4, 16, 128), BF),
            pltpu.VMEM((4, 3, 4, 4, 16, 128), BF),
            pltpu.VMEM((4, 4, 4, 16, 128), BF),
            pltpu.VMEM((4, 3, 4, 16, 128), BF),
            pltpu.VMEM((4, 4, 16, 128), BF),
            pltpu.VMEM((4, 3, 16, 128), BF),
            dma((52,)), dma((52,)), dma((7,)), dma((7,)), dma((6,)), dma((6,)),
            dma((4,)), dma((4,)), dma((36,)), dma((36,)),
        ],
        compiler_params=pltpu.CompilerParams(
            collective_id=0, has_side_effects=True, vmem_limit_bytes=56 * 1024 * 1024
        ),
        name="block",
    )(
        flat, grad, region_ids, w_qkv, w_proj,
        jnp.asarray(cut, BF), jnp.asarray(cut.T, BF), jnp.asarray(pick, BF), jnp.asarray(pick.T, BF),
    )
    block_out, grad_fields, qo, po = pl.pallas_call(
        settle,
        out_shape=(shape((tokens, C), BF), shape((tokens, C), BF), shape((12, C), F32), shape((4, C), F32)),
        in_specs=[anywhere] * 4,
        out_specs=[anywhere] * 4,
        scratch_shapes=[
            pltpu.VMEM((tokens, C), BF),
            pltpu.VMEM((tokens, C), BF),
            pltpu.VMEM((12, C), F32),
            pltpu.VMEM((4, C), F32),
            dma((10,)),
            dma((10,)),
        ],
        compiler_params=pltpu.CompilerParams(vmem_limit_bytes=56 * 1024 * 1024),
        name="settle",
    )(fo, go, qo, po)
    block_out = block_out.reshape(24, 3, 24, C).transpose(0, 2, 1, 3)
    grad_fields = grad_fields.reshape(24, 3, 24, C).transpose(0, 2, 1, 3)
    return block_out, grad_fields, qo, po


def solution(mesh):
    return jax.shard_map(
        shards,
        mesh=mesh,
        in_specs=(
            P("lat", "lon", None, None), P("lat"), P(("lon", "lat"), None), P(("lon", "lat"), None),
            P("lat", "lon", None, None),
        ),
        out_specs=(
            P("lat", "lon", None, None), P("lat", "lon", None, None),
            P(("lon", "lat"), None), P(("lon", "lat"), None),
        ),
        check_vma=False,
    )
```
